128 devices in a mesh: depth: 16 (over y, x), row: 2 (over core), col: 4 (over z).
Axes of the slice: x: 4, y: 4, z: 4, core: 2. Of those that a mesh axis runs over, the one named last changes fastest.
Arguments:
- inputs: bfloat16 [8192, 6144], P(('depth', 'col'), 'row'), may hold values from -6 to 6
- norm_gain: float32 [6144], P('row'), may hold values from 0.25 to 4, as said below
- w_qkv: bfloat16 [6144, 9216], P(('row', 'depth'), 'col'), as said below
- w_out: bfloat16 [3072, 6144], P(('col', 'depth'), 'row'), may hold values from -0.109375 to 0.109375
- segment_ids: int32 [16, 512], P('depth', 'row'), may hold values from 0 to 33, never falling along the last dimension, each value on 1 to 256 neighbouring positions
- cotangent: bfloat16 [8192, 6144], P(('depth', 'col'), 'row'), may hold values from -6 to 6
Outputs:
- branch_out: bfloat16 [8192, 6144], P(('depth', 'col'), 'row')
- grad_inputs: float32 [8192, 6144], P(('depth', 'col'), 'row')
- grad_gain: float32 [6144], P('row')
- grad_qkv: float32 [6144, 9216], P(('row', 'depth'), 'col')
- grad_out: float32 [3072, 6144], P(('col', 'depth'), 'row')
The draws below stay inside these ranges and needn't reach their ends.
Inputs may be any that keep to these rules, and one draw needn't show every extreme that they name: `segment_ids`: along each group's row the ids never fall; each image holds 1 to 256 tokens and one holds exactly that many. Attention joins only tokens of one group with equal ids. `norm_gain`: positive gains. `w_qkv`: projection weights of order 6144 ** -0.5.
All inputs are finite; a program needn't handle non-finite values.
Results may differ from the reference program's by a relative error of at most 0.029.
Values may be sent and summed in bfloat16 or wider, within the bound.
A program may use at most 192 MiB of HBM per device.

```python
import math
import jax
import jax.numpy as jnp
import numpy as np
from jax import lax

D = 6144
HD = 128
HEADS = 24
GROUP_TOK = 512
TOKENS = 8192
IMAGES = 34
N_DEPTH = 16
N_ROW = 2
N_COL = 4


def draw_norm_gain(key, part):
    key = jax.random.fold_in(key, 5)
    position = jnp.arange(D, dtype=jnp.float32) / (D - 1)
    low = 0.4
    rise = 8.0
    rough = jax.random.uniform(key, (D,), jnp.float32, 0.8, 1.2)
    return low * jnp.exp(jnp.log(rise) * position) * rough


def draw_w_qkv(key, part):
    key = jax.random.fold_in(key, 9)
    first, second = jax.random.split(key)
    columns = 3 * HEADS * HD
    entries = jnp.clip(jax.random.normal(first, (D, columns), jnp.float32), -6.0, 6.0)
    shared = 0.5 * jnp.clip(jax.random.normal(second, (1, columns), jnp.float32), -6.0, 6.0)
    return ((entries + shared) / jnp.sqrt(jnp.float32(D))).astype(jnp.bfloat16)


def steps_of(stream_key, extent, shards, low, high):
    loudness, own = 1.0, jax.random.fold_in(stream_key, 6)
    for axis_at, shards_of in shards:
        draws = jnp.exp(jax.random.uniform(jax.random.fold_in(own, axis_at), (shards_of,), jnp.float32, low / len(shards), high / len(shards)))
        loudness = loudness * jnp.repeat(draws, extent[axis_at] // shards_of).reshape([-1 if axis == axis_at else 1 for axis in range(len(extent))])
    return loudness


def split_up(number_of, total, bound, skew):
    portions = [(1 << 20) // math.isqrt(grade ** skew) + 1 for grade in range(2, number_of + 1)]
    spare, given = total - bound - (number_of - 1), [1] * (number_of - 1)
    while spare > 0:
        free = [i for i in range(number_of - 1) if given[i] < bound]
        whole, left = sum([portions[i] for i in free]), spare
        for i in free:
            addition = min(bound - given[i], max(1, left * portions[i] // whole), spare)
            given[i] = given[i] + addition
            spare = spare - addition
    return np.array([bound] + given)


def uneven(rng, number_of, total, reach, skew):
    if number_of == 2:
        one = jax.random.randint(rng, (), max(1, total - reach), min(reach, total - 1) + 1)
        return jnp.stack([one, total - one])
    lengths = jnp.asarray(split_up(number_of, total, reach, skew), jnp.int32)
    twos = (number_of - 1) // 2
    source_of, receiver = lengths[1:1 + 2 * twos:2], lengths[2:2 + 2 * twos:2]
    room = jnp.minimum(source_of - 1, reach - receiver)
    moved = jax.random.randint(jax.random.fold_in(rng, 1), (twos,), 0, 1 << 20) % (room + 1)
    lengths = lengths.at[1:1 + 2 * twos:2].set(source_of - moved).at[2:2 + 2 * twos:2].set(receiver + moved)
    return lengths[jax.random.permutation(jax.random.fold_in(rng, 2), number_of)]


def scatter_about(stream_key, dims, scale, reach, cuts=(), kind=jnp.bfloat16):
    factor_of = steps_of(stream_key, dims, cuts, -0.22, 0.18) if cuts else 1.0
    array = jax.random.normal(stream_key, dims, jnp.float32) * scale * factor_of
    return jnp.minimum(jnp.maximum(array, -reach), reach).astype(kind)


def setup_inputs(seed: int = 0) -> dict:
    key_list = jax.random.split(jax.random.key(seed), 7)
    return {
        "inputs": scatter_about(key_list[0], (TOKENS, D), 1.0, 6.0, ((0, 64), (1, 2))),
        "norm_gain": draw_norm_gain(jax.random.fold_in(key_list[6], 71), 0),
        "w_qkv": draw_w_qkv(jax.random.fold_in(key_list[6], 71), 0),
        "w_out": scatter_about(key_list[3], (HEADS * HD, D), (HEADS * HD) ** -0.5, 0.109375, ((0, 64), (1, 2))),
        "segment_ids": jax.vmap(lambda own: jnp.searchsorted(jnp.cumsum(uneven(own, IMAGES, GROUP_TOK, GROUP_TOK // 2, 2)), jnp.arange(GROUP_TOK), side="right"))(jax.random.split(key_list[4], N_DEPTH)).reshape((N_DEPTH, GROUP_TOK)).astype(jnp.int32),
        "cotangent": scatter_about(key_list[5], (TOKENS, D), 1.0, 6.0, ((0, 64), (1, 2))),
    }


EPSILON = 1e-06

def head_norm(values):
    centre = values - lax.optimization_barrier(jnp.mean(values, axis=-1, keepdims=True))
    spread = lax.optimization_barrier(jnp.mean(centre * centre, axis=-1, keepdims=True))
    return centre * lax.rsqrt(spread + EPSILON)

def rounded(values):
    return lax.optimization_barrier(values.astype(jnp.bfloat16)).astype(jnp.float32)

def split_sum(left, right, blocks):
    width = left.shape[1] // blocks

    def add_block(total, index):
        left_part = lax.dynamic_slice_in_dim(left, index * width, width, 1)
        right_part = lax.dynamic_slice_in_dim(right, index * width, width, 0)
        return (total + rounded(jnp.dot(left_part, right_part, preferred_element_type=jnp.float32)), None)
    start_total = jnp.zeros((left.shape[0], right.shape[1]), jnp.float32)
    return lax.scan(add_block, start_total, jnp.arange(blocks, dtype=jnp.int32))[0]

def query_split(left, right, blocks, factor):
    height = right.shape[0] // blocks

    def add_block(total, index):
        left_part = lax.dynamic_slice_in_dim(left, index * height, height, 1).astype(jnp.float32)
        right_part = lax.dynamic_slice_in_dim(right, index * height, height, 0).astype(jnp.float32)
        return (total + rounded(jnp.einsum('hqk,qhd->khd', left_part, right_part) * factor), None)
    start_total = jnp.zeros((left.shape[2], right.shape[1], right.shape[2]), jnp.float32)
    return lax.scan(add_block, start_total, jnp.arange(blocks, dtype=jnp.int32))[0]

def group_pass(inputs, cotangent, group_ids, norm_gain, w_qkv, w_out):
    tokens = inputs.shape[0]
    score_scale = 1.0 / math.sqrt(HD)
    as_float = inputs.astype(jnp.float32)
    average = lax.optimization_barrier(jnp.mean(as_float, axis=-1, keepdims=True))
    variance = lax.optimization_barrier(jnp.mean(as_float * as_float, axis=-1, keepdims=True)) - average * average
    inv_scale = lax.rsqrt(variance + EPSILON)
    normed_hat = (as_float - average) * inv_scale
    normed = (normed_hat * norm_gain).astype(jnp.bfloat16)
    projected = split_sum(normed, w_qkv, N_ROW).reshape(tokens, HEADS, 3, HD)
    queries = projected[:, :, 0]
    keys_raw = projected[:, :, 1]
    query_hat = head_norm(queries).astype(jnp.bfloat16)
    key_hat = head_norm(keys_raw).astype(jnp.bfloat16)
    values = projected[:, :, 2].astype(jnp.bfloat16)
    same_image = group_ids[:, None] == group_ids[None, :]
    scores = jnp.einsum('qhd,khd->hqk', query_hat.astype(jnp.float32), key_hat.astype(jnp.float32)) * score_scale
    weights = jnp.where(same_image[None], jnp.exp(scores), 0.0)
    attn_probs = weights / lax.optimization_barrier(jnp.sum(weights, axis=-1, keepdims=True))
    probs_low = attn_probs.astype(jnp.bfloat16)
    attended = jnp.einsum('hqk,khd->qhd', probs_low.astype(jnp.float32), values.astype(jnp.float32)).astype(jnp.bfloat16)
    attended_flat = attended.reshape(tokens, HEADS * HD)
    branch = split_sum(attended_flat, w_out, N_COL).astype(jnp.bfloat16)
    grad_attended = split_sum(cotangent, w_out.T, N_ROW).astype(jnp.bfloat16)
    grad_heads = grad_attended.reshape(tokens, HEADS, HD)
    out_part = jnp.dot(attended_flat.T, cotangent, preferred_element_type=jnp.float32)
    out_dot = lax.optimization_barrier(jnp.sum(grad_heads.astype(jnp.float32) * attended.astype(jnp.float32), axis=-1))
    grad_probs = jnp.einsum('qhd,khd->hqk', grad_heads.astype(jnp.float32), values.astype(jnp.float32))
    grad_scores = attn_probs * (grad_probs - out_dot.T[:, :, None])
    grad_low = grad_scores.astype(jnp.bfloat16)
    grad_query_hat = jnp.einsum('hqk,khd->qhd', grad_low.astype(jnp.float32), key_hat.astype(jnp.float32)) * score_scale
    grad_key_hat = query_split(grad_low, query_hat, N_ROW, score_scale)
    grad_values = query_split(probs_low, grad_heads, N_ROW, 1.0)
    grad_queries = jax.vjp(head_norm, queries)[1](grad_query_hat)[0]
    grad_keys = jax.vjp(head_norm, keys_raw)[1](grad_key_hat)[0]
    grad_projected = jnp.stack([grad_queries, grad_keys, grad_values], axis=2)
    grad_projected = grad_projected.reshape(tokens, 3 * HEADS * HD).astype(jnp.bfloat16)
    grad_normed = split_sum(grad_projected, w_qkv.T, N_COL)
    qkv_part = jnp.dot(normed.T, grad_projected, preferred_element_type=jnp.float32)
    grad_hat = grad_normed * norm_gain
    first_mean = lax.optimization_barrier(jnp.mean(grad_hat, axis=-1, keepdims=True))
    second_mean = lax.optimization_barrier(jnp.mean(grad_hat * normed_hat, axis=-1, keepdims=True))
    grad_inputs = inv_scale * (grad_hat - first_mean - normed_hat * second_mean)
    gain_part = lax.optimization_barrier(jnp.sum(grad_normed * normed_hat, axis=0))
    return (branch, grad_inputs, qkv_part, out_part, gain_part)

def reference(inputs, norm_gain, w_qkv, w_out, segment_ids, cotangent):
    grouped = inputs.reshape(N_DEPTH, GROUP_TOK, D)
    grouped_cot = cotangent.reshape(N_DEPTH, GROUP_TOK, D)

    def one_group(carry, items):
        group_in, group_cot, group_ids = items
        branch, grad_in, qkv_part, out_part, gain_part = group_pass(group_in, group_cot, group_ids, norm_gain, w_qkv, w_out)
        qkv_total, out_total, gain_total = carry
        return ((qkv_total + rounded(qkv_part), out_total + rounded(out_part), gain_total + gain_part), (branch, grad_in))
    start_carry = (jnp.zeros((D, 3 * HEADS * HD), jnp.float32), jnp.zeros((HEADS * HD, D), jnp.float32), jnp.zeros((D,), jnp.float32))
    totals, outputs = lax.scan(one_group, start_carry, (grouped, grouped_cot, segment_ids))
    qkv_total, out_total, gain_total = totals
    branch, grad_in = outputs
    return (branch.reshape(TOKENS, D), grad_in.reshape(TOKENS, D), gain_total, qkv_total, out_total)
```

```python
import math

import jax
import jax.numpy as jnp
from jax import lax
from jax.experimental import pallas as pl
from jax.experimental.pallas import tpu as pltpu
from jax.sharding import PartitionSpec as P

HD = 128
EPSILON = 1e-06
SCALE = 1.0 / math.sqrt(HD)
F32 = jnp.float32
BF16 = jnp.bfloat16
N_SEM = 240


def mm(a, b, ca=1, cb=0):
    return lax.dot_general(a, b, (((ca,), (cb,)), ((), ())), preferred_element_type=F32)


def norm_parts(v):
    centre = v - jnp.mean(v, axis=-1, keepdims=True)
    rs = lax.rsqrt(jnp.mean(centre * centre, axis=-1, keepdims=True) + EPSILON)
    return centre * rs, rs


def norm_back(hat, rs, g):
    dc = rs * (g - hat * jnp.mean(g * hat, axis=-1, keepdims=True))
    return dc - jnp.mean(dc, axis=-1, keepdims=True)


def kernel(
    x_in, gain, w_in, wo_in, ids_row, ids_col, cot_in,
    branch_out, gin_out, gain_out, gqkv_out, gout_out,
    wq, wo, rb, pb, normed, cot, gn, bpart, zb_buf, zg_buf,
    acc, psend, precv, gsend, grecv, gatt, att, gp,
    khat, vals, dk, dv, idr, idc, stat_s, stat_r, avg, inv, sum_s, sum_r,
    gain8, gain_s, gain_r,
    ssem, rsem, lsem, free,
):
    depth = lax.axis_index("depth")
    r = lax.axis_index("row")
    z = lax.axis_index("col")
    y, x = depth // 4, depth % 4
    coord = {"x": x, "y": y, "z": z}
    counter = [0]

    def alloc():
        counter[0] += 1
        return counter[0] - 1

    def dev(ax, i):
        if ax == "x":
            return {"depth": y * 4 + i}
        if ax == "y":
            return {"depth": i * 4 + x}
        if ax == "z":
            return {"col": i}
        return {"row": 1 - r}

    def rcopy(src, dst, k, device):
        return pltpu.make_async_remote_copy(
            src_ref=src, dst_ref=dst, send_sem=ssem.at[k], recv_sem=rsem.at[k],
            device_id=device, device_id_type=pl.DeviceIdType.MESH,
        )

    def nb(ax):
        i = coord[ax]
        return i, lax.rem(i + 1, 4), lax.rem(i + 3, 4), lax.rem(i + 2, 4)

    ring_nbrs = []
    for ax in ("x", "y"):
        _, up, dn, _ = nb(ax)
        ring_nbrs += [dev(ax, up), dev(ax, dn)]
    _, zup, zdn, _ = nb("z")
    all_nbrs = ring_nbrs + [dev("z", zup), dev("z", zdn), dev("r", None)]
    barrier = pltpu.get_barrier_semaphore()
    for d in all_nbrs:
        pl.semaphore_signal(barrier, inc=1, device_id=d, device_id_type=pl.DeviceIdType.MESH)

    local = []

    def lcopy(src, dst):
        c = pltpu.make_async_copy(src, dst, lsem.at[len(local)])
        c.start()
        local.append(c)

    for p in range(4):
        lcopy(wo_in.at[:, pl.ds(p * 768, 768)], wo.at[p, y, x])
    for c in range(3):
        lcopy(w_in.at[:, :, pl.ds(c * 384, 384)], wq.at[c, y, x, :, :, pl.ds(0, 384)])
        lcopy(w_in.at[:, :, pl.ds((3 + c) * 384, 384)], wq.at[c, y, x, :, :, pl.ds(384, 384)])
    lcopy(cot_in, cot.at[z])
    pl.semaphore_wait(barrier, len(all_nbrs))

    def ring_gather(ax, blk, p0, p1):
        i, up, dn, op = nb(ax)
        to_up, to_dn = dev(ax, up), dev(ax, dn)
        k = [alloc() for _ in range(6)]
        sent = []

        def go(b, kk, device):
            c = rcopy(b, b, kk, device)
            c.start()
            sent.append(c)

        def got(b, kk, device):
            rcopy(b, b, kk, device).wait_recv()

        go(blk(p0, i), k[0], to_up)
        go(blk(p1, i), k[1], to_dn)
        go(blk(p1, i), k[2], to_up)
        go(blk(p0, i), k[3], to_dn)
        yield
        got(blk(p0, dn), k[0], to_up)
        go(blk(p0, dn), k[4], to_up)
        got(blk(p1, up), k[1], to_dn)
        go(blk(p1, up), k[5], to_dn)
        yield
        got(blk(p1, dn), k[2], to_up)
        got(blk(p0, up), k[3], to_dn)
        got(blk(p0, op), k[4], to_up)
        got(blk(p1, op), k[5], to_dn)
        for c in sent:
            c.wait_send()
        yield

    def over(ref, f):
        if len(ref.shape) == 3:
            @pl.loop(0, ref.shape[0])
            def _(j):
                f(j)
        else:
            rows = 16

            @pl.loop(0, ref.shape[0] // rows)
            def _(j):
                f(pl.ds(pl.multiple_of(j * rows, rows), rows))

    def add_into(dst, src):
        def f(j):
            dst[j] = (dst[j].astype(F32) + src[j].astype(F32)).astype(BF16)
        over(dst, f)

    def ring_scatter(ax, blk, p0, p1, buf, emit):
        i, up, dn, op = nb(ax)
        to_up, to_dn = dev(ax, up), dev(ax, dn)
        k = [alloc() for _ in range(6)]
        sent = []

        def go(b, n, device):
            c = rcopy(b, buf(n), k[n], device)
            c.start()
            sent.append(c)

        def got(n, device):
            rcopy(buf(n), buf(n), k[n], device).wait_recv()

        go(blk(p0, op), 0, to_up)
        go(blk(p1, op), 1, to_dn)
        go(blk(p1, up), 2, to_up)
        go(blk(p0, dn), 3, to_dn)
        yield
        got(0, to_up)
        add_into(blk(p0, up), buf(0))
        go(blk(p0, up), 4, to_up)
        got(1, to_dn)
        add_into(blk(p1, dn), buf(1))
        go(blk(p1, dn), 5, to_dn)
        yield
        for n, device in ((2, to_up), (3, to_dn), (4, to_up), (5, to_dn)):
            got(n, device)
        emit(p0, blk(p0, i), buf(3), buf(4))
        emit(p1, blk(p1, i), buf(2), buf(5))
        for c in sent:
            c.wait_send()
        yield

    def piece(u, p, yy, xx):
        return wo.at[p, yy, xx] if u == 0 else wq.at[u - 1, yy, xx, p]

    def rowblk(u, p, yy):
        return wo.at[p, yy] if u == 0 else wq.at[u - 1, yy, :, p]

    def colblk(u, p, xx):
        return wo.at[p, :, xx] if u == 0 else wq.at[u - 1, :, xx, p]

    def both(a, b):
        for _ in range(3):
            next(a)
            next(b)
            yield

    def small_gather(u):
        return both(
            ring_gather("x", lambda p, i: piece(u, p, y, i), 0, 1),
            ring_gather("y", lambda p, i: piece(u, p, i, x), 2, 3),
        )

    def big_gather(u):
        return both(
            ring_gather("y", lambda p, i: rowblk(u, p, i), 0, 1),
            ring_gather("x", lambda p, i: colblk(u, p, i), 2, 3),
        )

    def emit_sum(p, own, a, b):
        def f(j):
            own[j] = (own[j].astype(F32) + a[j].astype(F32) + b[j].astype(F32)).astype(BF16)
        over(own, f)

    def big_scatter(u, slot):
        return both(
            ring_scatter("y", lambda p, i: rowblk(u, p, i), 0, 1, lambda n: rb.at[slot, n], emit_sum),
            ring_scatter("x", lambda p, i: colblk(u, p, i), 2, 3, lambda n: rb.at[slot, 6 + n], emit_sum),
        )

    def small_scatter(u):
        def emit(p, own, a, b):
            def f(j):
                total = own[j].astype(F32) + a[j].astype(F32) + b[j].astype(F32)
                if u == 0:
                    gout_out[j, p * 768:(p + 1) * 768] = total
                else:
                    c = u - 1
                    gqkv_out[p, j, c * 384:(c + 1) * 384] = total[:, :384]
                    gqkv_out[p, j, (3 + c) * 384:(4 + c) * 384] = total[:, 384:]
            over(own, f)

        return both(
            ring_scatter("x", lambda p, i: piece(u, p, y, i), 0, 1, lambda n: pb.at[u, n], emit),
            ring_scatter("y", lambda p, i: piece(u, p, i, x), 2, 3, lambda n: pb.at[u, 6 + n], emit),
        )

    def partner_copy(src, dst):
        c = rcopy(src, dst, alloc(), dev("r", None))
        c.start()
        return c

    def ln_stats():
        @pl.loop(0, 4)
        def _(t):
            rows = pl.ds(pl.multiple_of(t * 32, 32), 32)
            v = x_in[rows, :].astype(F32)
            stat_s[rows, :128] = jnp.broadcast_to(jnp.sum(v, axis=1, keepdims=True), (32, 128))
            stat_s[rows, 128:] = jnp.broadcast_to(jnp.sum(v * v, axis=1, keepdims=True), (32, 128))
        return partner_copy(stat_s, stat_r)

    def ln_apply(copy):
        copy.wait()
        total = stat_s[...] + stat_r[...]
        average = total[:, :128] / 6144.0
        variance = total[:, 128:] / 6144.0 - average * average
        avg[...] = average
        inv[...] = lax.rsqrt(variance + EPSILON)

        @pl.loop(0, 2)
        def _(p):
            @pl.loop(0, 2)
            def _(t):
                rows = pl.ds(pl.multiple_of(p * 64 + t * 32, 32), 32)
                v = x_in[rows, :].astype(F32)
                hat = (v - avg[rows, :1]) * inv[rows, :1]
                normed[z, p, pl.ds(pl.multiple_of(t * 32, 32), 32), :] = (hat * gain[...]).astype(BF16)

    def lanes(start, size):
        return pl.ds(pl.multiple_of(start, 128), size)

    def gatt_part(who):
        acc[...] = jnp.zeros_like(acc)

        @pl.loop(0, 4)
        def _(cb):
            left = cot[:, :, :, lanes(cb * 768, 768)].reshape(512, 768)
            right = wo[cb, pl.ds(2 * who, 2)].reshape(384, 768)
            acc[...] += mm(left, right, 1, 1)

    def gatt_first():
        gatt_part(1 - r)
        gsend[...] = acc[...].astype(BF16)
        c = partner_copy(gsend, grecv)
        gatt_part(r)
        return c

    def gatt_last(c):
        c.wait()
        gatt[...] = (acc[...] + grecv[...].astype(F32)).astype(BF16)

    def proj_part(c, who):
        acc[...] = jnp.zeros_like(acc)

        @pl.loop(0, 4)
        def _(k):
            left = normed[:, :, :, lanes(k * 768, 768)].reshape(512, 768)
            right = wq[c, k, :, :, :, lanes(who * 384, 384)].reshape(768, 384)
            acc[...] += mm(left, right)

    def proj_a(c):
        proj_part(c, 1 - r)
        psend[c] = acc[...].astype(BF16)
        return partner_copy(psend.at[c], precv.at[c])

    def proj_b(c):
        proj_part(c, r)

    def attention(c, copy):
        copy.wait()
        acc[...] += precv[c].astype(F32)
        hat, _ = norm_parts(acc[:, 128:256])
        khat[...] = hat.astype(BF16)
        vals[...] = acc[:, 256:].astype(BF16)
        dk[...] = jnp.zeros_like(dk)
        dv[...] = jnp.zeros_like(dv)
        head = lanes((3 * r + c) * 128, 128)
        base = pl.multiple_of(r * 384, 128)

        @pl.loop(0, 4)
        def _(t):
            rows = pl.ds(pl.multiple_of(t * 128, 128), 128)
            qh, rs = norm_parts(acc[rows, :128])
            ql = qh.astype(BF16)
            ids = jnp.concatenate([idr[0], idr[1]], axis=1)
            same = idc[t][:, :1] == ids
            weights = jnp.where(same, jnp.exp(mm(ql, khat[...], 1, 1) * SCALE), 0.0)
            probs = weights * (1.0 / jnp.sum(weights, axis=-1, keepdims=True))
            low = probs.astype(BF16)
            out = mm(low, vals[...]).astype(BF16)
            att[rows, head] = out
            go = gatt[rows, c * 128:(c + 1) * 128]
            dot = jnp.sum(go.astype(F32) * out.astype(F32), axis=-1, keepdims=True)
            gl = (probs * (mm(go, vals[...], 1, 1) - dot)).astype(BF16)
            dq = mm(gl, khat[...]) * SCALE
            dk[...] += mm(gl, ql, 0, 0)
            dv[...] += mm(low, go, 0, 0)
            gp[c, rows, pl.ds(base, 128)] = norm_back(qh, rs, dq).astype(BF16)

        hat, rs = norm_parts(acc[:, 128:256])
        gp[c, :, pl.ds(pl.multiple_of(base + 128, 128), 128)] = norm_back(hat, rs, dk[...] * SCALE).astype(BF16)
        gp[c, :, pl.ds(pl.multiple_of(base + 256, 128), 128)] = dv[...].astype(BF16)
        mine = gp.at[c, :, pl.ds(base, 384)]
        return partner_copy(mine, mine), partner_copy(att.at[:, head], att.at[:, head])

    def weight_grad(c, first, last):
        @pl.loop(first, last)
        def _(f):
            yy, x0 = f // 2, (f % 2) * 2
            right = wq[c, yy, pl.ds(x0, 2)].reshape(384, 768)
            cols = lanes(f * 384, 384)
            part = mm(gp[c], right, 1, 1).reshape(4, 2, 64, 384)
            if c > 0:
                part = part + gn[:, :, :, cols].astype(F32)
            gn[:, :, :, cols] = part.astype(BF16)
            left = normed[:, :, :, cols].reshape(512, 384)
            wq[c, yy, pl.ds(x0, 2)] = mm(left, gp[c], 0, 0).astype(BF16).reshape(2, 4, 48, 768)

    def out_grad():
        @pl.loop(0, 4)
        def _(cb):
            cols = lanes(cb * 768, 768)
            bpart[:, :, :, cols] = mm(att[...], wo[cb].reshape(768, 768)).astype(BF16).reshape(4, 2, 64, 768)
            right = cot[:, :, :, cols].reshape(512, 768)
            wo[cb] = mm(att[...], right, 0, 0).astype(BF16).reshape(4, 4, 48, 768)

    def release(n):
        for d in ring_nbrs:
            pl.semaphore_signal(free.at[n], inc=1, device_id=d, device_id_type=pl.DeviceIdType.MESH)

    def acquire(n):
        pl.semaphore_wait(free.at[n], 4)

    def emit_branch(p, own, a, b):
        def f(j):
            total = own[j].astype(F32) + a[j].astype(F32) + b[j].astype(F32)
            branch_out[p, j] = total.astype(BF16)
        over(own, f)

    def emit_gn(p, own, a, b):
        def f(j):
            gin_out[p, j] = own[j].astype(F32) + a[j].astype(F32) + b[j].astype(F32)
        over(own, f)

    def ln_back_first():
        gain8[...] = jnp.zeros_like(gain8)

        @pl.loop(0, 2)
        def _(p):
            @pl.loop(0, 4)
            def _(t):
                rows = pl.ds(pl.multiple_of(p * 64 + t * 16, 16), 16)
                part = pl.ds(pl.multiple_of(t * 16, 16), 16)
                hat = (x_in[rows, :].astype(F32) - avg[rows, :1]) * inv[rows, :1]
                g = gin_out[p, part, :]
                gh = g * hat
                gain8[...] += gh.reshape(2, 8, 3072).sum(0)
                sum_s[rows, :128] = jnp.broadcast_to(jnp.sum(g * gain[...], axis=1, keepdims=True), (16, 128))
                sum_s[rows, 128:] = jnp.broadcast_to(jnp.sum(gh * gain[...], axis=1, keepdims=True), (16, 128))
        c = partner_copy(sum_s, sum_r)
        gain_s[0] = jnp.sum(gain8[...], axis=0, keepdims=True)
        return c

    def ln_back_last(c):
        c.wait()
        sum_r[...] = (sum_s[...] + sum_r[...]) / 6144.0

        @pl.loop(0, 2)
        def _(p):
            @pl.loop(0, 4)
            def _(t):
                rows = pl.ds(pl.multiple_of(p * 64 + t * 16, 16), 16)
                part = pl.ds(pl.multiple_of(t * 16, 16), 16)
                hat = (x_in[rows, :].astype(F32) - avg[rows, :1]) * inv[rows, :1]
                g = gin_out[p, part, :] * gain[...]
                gin_out[p, part, :] = inv[rows, :1] * (g - sum_r[rows, :1] - hat * sum_r[rows, 128:129])

    def gain_reduce():
        step = 0
        for ax in ("z", "x", "y"):
            i = coord[ax]
            for other in (i + 1 - 2 * (i % 2), 3 - i):
                c = rcopy(gain_s.at[step], gain_r.at[step], alloc(), dev(ax, other))
                c.start()
                yield
                c.wait()
                gain_s[step + 1] = gain_s[step] + gain_r[step]
                step += 1
        gain_out[...] = gain_s[step]
        yield

    sg = [small_gather(u) for u in range(4)]
    bg = [big_gather(u) for u in range(4)]
    z_cot = ring_gather("z", lambda p, i: cot.at[i, p], 0, 1)
    z_normed = ring_gather("z", lambda p, i: normed.at[i, p], 0, 1)

    for c in local:
        c.wait()
    next(sg[0])
    next(z_cot)
    next(sg[1])
    idr[r] = ids_row[...]
    idc[pl.ds(2 * r, 2)] = ids_col[...]
    ids_a = partner_copy(idr.at[r], idr.at[r])
    ids_b = partner_copy(idc.at[pl.ds(2 * r, 2)], idc.at[pl.ds(2 * r, 2)])
    stats = ln_stats()
    next(sg[0])
    next(sg[1])
    ln_apply(stats)
    next(sg[0])
    next(bg[0])
    next(sg[2])
    next(z_cot)
    next(z_normed)
    next(sg[1])
    next(bg[0])
    next(sg[2])
    next(bg[1])
    next(z_cot)
    next(bg[0])
    next(sg[3])
    gcopy = gatt_first()
    next(z_normed)
    next(sg[2])
    next(bg[1])
    next(sg[3])
    next(bg[2])
    gatt_last(gcopy)
    ids_a.wait()
    ids_b.wait()
    next(z_normed)
    next(sg[3])
    next(bg[1])

    pc = proj_a(0)
    next(bg[2])
    proj_b(0)
    next(bg[3])
    ex0 = attention(0, pc)
    next(bg[2])
    for e in ex0:
        e.wait()
    weight_grad(0, 0, 4)
    next(bg[3])
    weight_grad(0, 4, 8)
    rs0, ps0 = big_scatter(1, 0), small_scatter(1)
    rs1, ps1 = big_scatter(2, 1), small_scatter(2)
    rs2, ps2 = big_scatter(0, 0), small_scatter(0)
    rs3, ps3 = big_scatter(3, 1), small_scatter(3)
    next(rs0)
    pc = proj_a(1)
    proj_b(1)
    next(rs0)
    ex1 = attention(1, pc)
    next(bg[3])
    for e in ex1:
        e.wait()
    weight_grad(1, 0, 4)
    weight_grad(1, 4, 8)
    next(rs1)
    next(rs0)
    release(0)
    next(ps0)
    pc = proj_a(2)
    proj_b(2)
    next(rs1)
    next(ps0)
    ex2 = attention(2, pc)
    ex2[1].wait()
    out_grad()
    acquire(0)
    next(rs2)
    z_branch = ring_scatter("z", lambda p, i: bpart.at[i, p], 0, 1, lambda n: zb_buf.at[n], emit_branch)
    z_gn = ring_scatter("z", lambda p, i: gn.at[i, p], 0, 1, lambda n: zg_buf.at[n], emit_gn)
    next(z_branch)
    next(rs1)
    release(1)
    next(ps1)
    next(ps0)
    ex2[0].wait()
    weight_grad(2, 0, 4)
    next(rs2)
    next(ps1)
    weight_grad(2, 4, 8)
    acquire(1)
    next(rs3)
    next(z_branch)
    next(z_gn)
    next(rs2)
    next(ps2)
    next(ps1)
    next(rs3)
    next(ps2)
    next(z_branch)
    next(z_gn)
    next(rs3)
    next(ps3)
    next(ps2)
    next(z_gn)
    back = ln_back_first()
    reduce = gain_reduce()
    next(reduce)
    next(ps3)
    next(reduce)
    ln_back_last(back)
    for _ in range(5):
        next(reduce)
    next(ps3)


def shards(inputs, norm_gain, w_qkv, w_out, segment_ids, cotangent):
    own_ids = segment_ids[0]
    vmem = pl.BlockSpec(memory_space=pltpu.VMEM)
    hbm = pl.BlockSpec(memory_space=pl.ANY)
    V = pltpu.VMEM
    outs = pl.pallas_call(
        kernel,
        out_shape=(
            jax.ShapeDtypeStruct((2, 64, 3072), BF16),
            jax.ShapeDtypeStruct((2, 64, 3072), F32),
            jax.ShapeDtypeStruct((1, 3072), F32),
            jax.ShapeDtypeStruct((4, 48, 2304), F32),
            jax.ShapeDtypeStruct((48, 3072), F32),
        ),
        in_specs=[vmem, vmem, hbm, hbm, vmem, vmem, hbm],
        out_specs=(vmem,) * 5,
        scratch_shapes=[
            V((3, 4, 4, 4, 48, 768), BF16),
            V((4, 4, 4, 48, 768), BF16),
            V((2, 12, 4, 48, 768), BF16),
            V((4, 12, 48, 768), BF16),
            V((4, 2, 64, 3072), BF16),
            V((4, 2, 64, 3072), BF16),
            V((4, 2, 64, 3072), BF16),
            V((4, 2, 64, 3072), BF16),
            V((6, 64, 3072), BF16),
            V((6, 64, 3072), BF16),
            V((512, 384), F32),
            V((3, 512, 384), BF16),
            V((3, 512, 384), BF16),
            V((512, 384), BF16),
            V((512, 384), BF16),
            V((512, 384), BF16),
            V((512, 768), BF16),
            V((3, 512, 768), BF16),
            V((512, 128), BF16),
            V((512, 128), BF16),
            V((512, 128), F32),
            V((512, 128), F32),
            V((2, 1, 256), jnp.int32),
            V((4, 128, 128), jnp.int32),
            V((128, 256), F32),
            V((128, 256), F32),
            V((128, 128), F32),
            V((128, 128), F32),
            V((128, 256), F32),
            V((128, 256), F32),
            V((8, 3072), F32),
            V((7, 1, 3072), F32),
            V((6, 1, 3072), F32),
            pltpu.SemaphoreType.DMA((N_SEM,)),
            pltpu.SemaphoreType.DMA((N_SEM,)),
            pltpu.SemaphoreType.DMA((11,)),
            pltpu.SemaphoreType.REGULAR((2,)),
        ],
        compiler_params=pltpu.CompilerParams(
            collective_id=0, has_side_effects=True, vmem_limit_bytes=62 * 1024 * 1024
        ),
    )(
        inputs,
        norm_gain.reshape(1, 3072),
        w_qkv.reshape(4, 48, 2304),
        w_out,
        own_ids.reshape(1, 256),
        jnp.broadcast_to(own_ids.reshape(2, 128, 1), (2, 128, 128)),
        cotangent.reshape(2, 64, 3072),
    )
    branch, gin, gain, gqkv, gout = outs
    return (
        branch.reshape(128, 3072), gin.reshape(128, 3072), gain.reshape(3072),
        gqkv.reshape(192, 2304), gout,
    )


def solution(mesh):
    placed = (
        P(("depth", "col"), "row"),
        P("row"),
        P(("row", "depth"), "col"),
        P(("col", "depth"), "row"),
        P("depth", "row"),
        P(("depth", "col"), "row"),
    )
    return jax.shard_map(
        shards,
        mesh=mesh,
        in_specs=placed,
        out_specs=(
            P(("depth", "col"), "row"),
            P(("depth", "col"), "row"),
            P("row"),
            P(("row", "depth"), "col"),
            P(("col", "depth"), "row"),
        ),
        check_vma=False,
    )
```

```python
import math

import jax
import jax.numpy as jnp
from jax import lax
from jax.experimental import pallas as pl
from jax.experimental.pallas import tpu as pltpu
from jax.sharding import PartitionSpec as P

HD = 128
EPSILON = 1e-06
SCALE = 1.0 / math.sqrt(HD)
F32 = jnp.float32
BF16 = jnp.bfloat16
N_SEM = 240


def mm(a, b, ca=1, cb=0):
    return lax.dot_general(a, b, (((ca,), (cb,)), ((), ())), preferred_element_type=F32)


def norm_parts(v):
    centre = v - jnp.mean(v, axis=-1, keepdims=True)
    rs = lax.rsqrt(jnp.mean(centre * centre, axis=-1, keepdims=True) + EPSILON)
    return centre * rs, rs


def norm_back(hat, rs, g):
    dc = rs * (g - hat * jnp.mean(g * hat, axis=-1, keepdims=True))
    return dc - jnp.mean(dc, axis=-1, keepdims=True)


def kernel(
    x_hbm, gain, w_in, wo_in, ids_row, cot_in,
    branch_hbm, gin_hbm, gain_out, gqkv_hbm, gout_hbm,
    x_in, branch_out, gin_out, gqkv_out, gout_out,
    wq, wo, rb, pb, normed, cot, gn, bpart, zb_buf, zg_buf,
    acc, psend, precv, gsend, grecv, gatt, att, gp,
    khat, vals, dk, dv, idr, idc, stat_s, stat_r, avg, inv, sum_s, sum_r,
    gain8, gain_s, gain_r,
    ssem, rsem, lsem, osem, free,
):
    depth = lax.axis_index("depth")
    r = lax.axis_index("row")
    z = lax.axis_index("col")
    y, x = depth // 4, depth % 4
    coord = {"x": x, "y": y, "z": z}
    counter = [0]

    def alloc():
        counter[0] += 1
        return counter[0] - 1

    def dev(ax, i):
        if ax == "x":
            return {"depth": y * 4 + i}
        if ax == "y":
            return {"depth": i * 4 + x}
        if ax == "z":
            return {"col": i}
        return {"row": 1 - r}

    def rcopy(src, dst, k, device):
        return pltpu.make_async_remote_copy(
            src_ref=src, dst_ref=dst, send_sem=ssem.at[k], recv_sem=rsem.at[k],
            device_id=device, device_id_type=pl.DeviceIdType.MESH,
        )

    def nb(ax):
        i = coord[ax]
        return i, lax.rem(i + 1, 4), lax.rem(i + 3, 4), lax.rem(i + 2, 4)

    ring_nbrs = []
    for ax in ("x", "y"):
        _, up, dn, _ = nb(ax)
        ring_nbrs += [dev(ax, up), dev(ax, dn)]
    _, zup, zdn, _ = nb("z")
    all_nbrs = ring_nbrs + [dev("z", zup), dev("z", zdn), dev("r", None)]
    barrier = pltpu.get_barrier_semaphore()
    for d in all_nbrs:
        pl.semaphore_signal(barrier, inc=1, device_id=d, device_id_type=pl.DeviceIdType.MESH)

    local = []

    def lcopy(src, dst):
        c = pltpu.make_async_copy(src, dst, lsem.at[len(local)])
        c.start()
        local.append(c)

    for p in range(4):
        lcopy(wo_in.at[:, pl.ds(p * 768, 768)], wo.at[p, y, x])
    lcopy(cot_in, cot.at[z])
    lcopy(x_hbm, x_in)
    for c in range(3):
        lcopy(w_in.at[:, :, pl.ds(c * 384, 384)], wq.at[c, y, x, :, :, pl.ds(0, 384)])
        lcopy(w_in.at[:, :, pl.ds((3 + c) * 384, 384)], wq.at[c, y, x, :, :, pl.ds(384, 384)])
    pl.semaphore_wait(barrier, len(all_nbrs))

    def ring_gather(ax, blk, p0, p1):
        i, up, dn, op = nb(ax)
        to_up, to_dn = dev(ax, up), dev(ax, dn)
        k = [alloc() for _ in range(6)]
        sent = []

        def go(b, kk, device):
            c = rcopy(b, b, kk, device)
            c.start()
            sent.append(c)

        def got(b, kk, device):
            rcopy(b, b, kk, device).wait_recv()

        go(blk(p0, i), k[0], to_up)
        go(blk(p1, i), k[1], to_dn)
        go(blk(p1, i), k[2], to_up)
        go(blk(p0, i), k[3], to_dn)
        yield
        got(blk(p0, dn), k[0], to_up)
        go(blk(p0, dn), k[4], to_up)
        got(blk(p1, up), k[1], to_dn)
        go(blk(p1, up), k[5], to_dn)
        yield
        got(blk(p1, dn), k[2], to_up)
        got(blk(p0, up), k[3], to_dn)
        got(blk(p0, op), k[4], to_up)
        got(blk(p1, op), k[5], to_dn)
        for c in sent:
            c.wait_send()
        yield

    def over(ref, f):
        if len(ref.shape) == 3:
            @pl.loop(0, ref.shape[0])
            def _(j):
                f(j)
        else:
            rows = 16

            @pl.loop(0, ref.shape[0] // rows)
            def _(j):
                f(pl.ds(pl.multiple_of(j * rows, rows), rows))

    def add_into(dst, src):
        def f(j):
            dst[j] = (dst[j].astype(F32) + src[j].astype(F32)).astype(BF16)
        over(dst, f)

    def ring_scatter(ax, blk, p0, p1, buf, emit):
        i, up, dn, op = nb(ax)
        to_up, to_dn = dev(ax, up), dev(ax, dn)
        k = [alloc() for _ in range(6)]
        sent = []

        def go(b, n, device):
            c = rcopy(b, buf(n), k[n], device)
            c.start()
            sent.append(c)

        def got(n, device):
            rcopy(buf(n), buf(n), k[n], device).wait_recv()

        go(blk(p0, op), 0, to_up)
        go(blk(p1, op), 1, to_dn)
        go(blk(p1, up), 2, to_up)
        go(blk(p0, dn), 3, to_dn)
        yield
        got(0, to_up)
        add_into(blk(p0, up), buf(0))
        go(blk(p0, up), 4, to_up)
        got(1, to_dn)
        add_into(blk(p1, dn), buf(1))
        go(blk(p1, dn), 5, to_dn)
        yield
        for n, device in ((2, to_up), (3, to_dn), (4, to_up), (5, to_dn)):
            got(n, device)
        emit(p0, blk(p0, i), buf(3), buf(4))
        emit(p1, blk(p1, i), buf(2), buf(5))
        for c in sent:
            c.wait_send()
        yield

    def piece(u, p, yy, xx):
        return wo.at[p, yy, xx] if u == 0 else wq.at[u - 1, yy, xx, p]

    def rowblk(u, p, yy):
        return wo.at[p, yy] if u == 0 else wq.at[u - 1, yy, :, p]

    def colblk(u, p, xx):
        return wo.at[p, :, xx] if u == 0 else wq.at[u - 1, :, xx, p]

    def both(a, b):
        for _ in range(3):
            next(a)
            next(b)
            yield

    def small_gather(u):
        return both(
            ring_gather("x", lambda p, i: piece(u, p, y, i), 0, 1),
            ring_gather("y", lambda p, i: piece(u, p, i, x), 2, 3),
        )

    def big_gather(u):
        return both(
            ring_gather("y", lambda p, i: rowblk(u, p, i), 0, 1),
            ring_gather("x", lambda p, i: colblk(u, p, i), 2, 3),
        )

    def emit_sum(p, own, a, b):
        def f(j):
            own[j] = (own[j].astype(F32) + a[j].astype(F32) + b[j].astype(F32)).astype(BF16)
        over(own, f)

    def big_scatter(u, slot):
        return both(
            ring_scatter("y", lambda p, i: rowblk(u, p, i), 0, 1, lambda n: rb.at[slot, n], emit_sum),
            ring_scatter("x", lambda p, i: colblk(u, p, i), 2, 3, lambda n: rb.at[slot, 6 + n], emit_sum),
        )

    def small_scatter(u):
        def emit(p, own, a, b):
            def f(j):
                total = own[j].astype(F32) + a[j].astype(F32) + b[j].astype(F32)
                if u == 0:
                    gout_out[j, p * 768:(p + 1) * 768] = total
                else:
                    c = u - 1
                    gqkv_out[p, j, c * 384:(c + 1) * 384] = total[:, :384]
                    gqkv_out[p, j, (3 + c) * 384:(4 + c) * 384] = total[:, 384:]
            over(own, f)

        return both(
            ring_scatter("x", lambda p, i: piece(u, p, y, i), 0, 1, lambda n: pb.at[u, n], emit),
            ring_scatter("y", lambda p, i: piece(u, p, i, x), 2, 3, lambda n: pb.at[u, 6 + n], emit),
        )

    def partner_copy(src, dst):
        c = rcopy(src, dst, alloc(), dev("r", None))
        c.start()
        return c

    def id_columns():
        for t in range(4):
            row = idr[t // 2][:, (t % 2) * 128:(t % 2 + 1) * 128].astype(F32)
            idc[t] = jnp.transpose(jnp.broadcast_to(row, (128, 128)))

    def ln_stats():
        @pl.loop(0, 4)
        def _(t):
            rows = pl.ds(pl.multiple_of(t * 32, 32), 32)
            v = x_in[rows, :].astype(F32)
            stat_s[rows, :128] = jnp.broadcast_to(jnp.sum(v, axis=1, keepdims=True), (32, 128))
            stat_s[rows, 128:] = jnp.broadcast_to(jnp.sum(v * v, axis=1, keepdims=True), (32, 128))
        return partner_copy(stat_s, stat_r)

    def ln_apply(copy):
        copy.wait()
        total = stat_s[...] + stat_r[...]
        average = total[:, :128] / 6144.0
        variance = total[:, 128:] / 6144.0 - average * average
        avg[...] = average
        inv[...] = lax.rsqrt(variance + EPSILON)

        @pl.loop(0, 2)
        def _(p):
            @pl.loop(0, 2)
            def _(t):
                rows = pl.ds(pl.multiple_of(p * 64 + t * 32, 32), 32)
                v = x_in[rows, :].astype(F32)
                hat = (v - avg[rows, :1]) * inv[rows, :1]
                normed[z, p, pl.ds(pl.multiple_of(t * 32, 32), 32), :] = (hat * gain[...]).astype(BF16)

    def lanes(start, size):
        return pl.ds(pl.multiple_of(start, 128), size)

    def gatt_part(who):
        acc[...] = jnp.zeros_like(acc)

        @pl.loop(0, 4)
        def _(cb):
            left = cot[:, :, :, lanes(cb * 768, 768)].reshape(512, 768)
            right = wo[cb, pl.ds(2 * who, 2)].reshape(384, 768)
            acc[...] += mm(left, right, 1, 1)

    def gatt_first():
        gatt_part(1 - r)
        gsend[...] = acc[...].astype(BF16)
        c = partner_copy(gsend, grecv)
        gatt_part(r)
        return c

    def gatt_last(c):
        c.wait()
        gatt[...] = (acc[...] + grecv[...].astype(F32)).astype(BF16)

    def proj_part(c, who):
        acc[...] = jnp.zeros_like(acc)

        @pl.loop(0, 4)
        def _(k):
            left = normed[:, :, :, lanes(k * 768, 768)].reshape(512, 768)
            right = wq[c, k, :, :, :, lanes(who * 384, 384)].reshape(768, 384)
            acc[...] += mm(left, right)

    def proj_a(c):
        proj_part(c, 1 - r)
        psend[c] = acc[...].astype(BF16)
        return partner_copy(psend.at[c], precv.at[c])

    def proj_b(c):
        proj_part(c, r)

    def attention(c, copy):
        copy.wait()
        acc[...] += precv[c].astype(F32)
        hat, _ = norm_parts(acc[:, 128:256])
        khat[...] = hat.astype(BF16)
        vals[...] = acc[:, 256:].astype(BF16)
        dk[...] = jnp.zeros_like(dk)
        dv[...] = jnp.zeros_like(dv)
        head = lanes((3 * r + c) * 128, 128)
        base = pl.multiple_of(r * 384, 128)

        @pl.loop(0, 4)
        def _(t):
            rows = pl.ds(pl.multiple_of(t * 128, 128), 128)
            qh, rs = norm_parts(acc[rows, :128])
            ql = qh.astype(BF16)
            ids = jnp.concatenate([idr[0], idr[1]], axis=1).astype(F32)
            same = idc[t][:, :1] == ids
            weights = jnp.where(same, jnp.exp(mm(ql, khat[...], 1, 1) * SCALE), 0.0)
            probs = weights * (1.0 / jnp.sum(weights, axis=-1, keepdims=True))
            low = probs.astype(BF16)
            out = mm(low, vals[...]).astype(BF16)
            att[rows, head] = out
            go = gatt[rows, c * 128:(c + 1) * 128]
            dot = jnp.sum(go.astype(F32) * out.astype(F32), axis=-1, keepdims=True)
            gl = (probs * (mm(go, vals[...], 1, 1) - dot)).astype(BF16)
            dq = mm(gl, khat[...]) * SCALE
            dk[...] += mm(gl, ql, 0, 0)
            dv[...] += mm(low, go, 0, 0)
            gp[c, rows, pl.ds(base, 128)] = norm_back(qh, rs, dq).astype(BF16)

        hat, rs = norm_parts(acc[:, 128:256])
        gp[c, :, pl.ds(pl.multiple_of(base + 128, 128), 128)] = norm_back(hat, rs, dk[...] * SCALE).astype(BF16)
        gp[c, :, pl.ds(pl.multiple_of(base + 256, 128), 128)] = dv[...].astype(BF16)
        mine = gp.at[c, :, pl.ds(base, 384)]
        return partner_copy(mine, mine), partner_copy(att.at[:, head], att.at[:, head])

    def weight_grad(c, first, last):
        @pl.loop(first, last)
        def _(f):
            yy, x0 = f // 2, (f % 2) * 2
            right = wq[c, yy, pl.ds(x0, 2)].reshape(384, 768)
            cols = lanes(f * 384, 384)
            part = mm(gp[c], right, 1, 1).reshape(4, 2, 64, 384)
            if c > 0:
                part = part + gn[:, :, :, cols].astype(F32)
            gn[:, :, :, cols] = part.astype(BF16)
            left = normed[:, :, :, cols].reshape(512, 384)
            wq[c, yy, pl.ds(x0, 2)] = mm(left, gp[c], 0, 0).astype(BF16).reshape(2, 4, 48, 768)

    def out_grad():
        @pl.loop(0, 4)
        def _(cb):
            cols = lanes(cb * 768, 768)
            bpart[:, :, :, cols] = mm(att[...], wo[cb].reshape(768, 768)).astype(BF16).reshape(4, 2, 64, 768)
            right = cot[:, :, :, cols].reshape(512, 768)
            wo[cb] = mm(att[...], right, 0, 0).astype(BF16).reshape(4, 4, 48, 768)

    def release(n):
        for d in ring_nbrs:
            pl.semaphore_signal(free.at[n], inc=1, device_id=d, device_id_type=pl.DeviceIdType.MESH)

    def acquire(n):
        pl.semaphore_wait(free.at[n], 4)

    def emit_branch(p, own, a, b):
        def f(j):
            total = own[j].astype(F32) + a[j].astype(F32) + b[j].astype(F32)
            branch_out[p, j] = total.astype(BF16)
        over(own, f)

    def emit_gn(p, own, a, b):
        def f(j):
            gin_out[p, j] = own[j].astype(F32) + a[j].astype(F32) + b[j].astype(F32)
        over(own, f)

    def ln_back_first():
        gain8[...] = jnp.zeros_like(gain8)

        @pl.loop(0, 2)
        def _(p):
            @pl.loop(0, 4)
            def _(t):
                rows = pl.ds(pl.multiple_of(p * 64 + t * 16, 16), 16)
                part = pl.ds(pl.multiple_of(t * 16, 16), 16)
                hat = (x_in[rows, :].astype(F32) - avg[rows, :1]) * inv[rows, :1]
                g = gin_out[p, part, :]
                gh = g * hat
                gain8[...] += gh.reshape(2, 8, 3072).sum(0)
                sum_s[rows, :128] = jnp.broadcast_to(jnp.sum(g * gain[...], axis=1, keepdims=True), (16, 128))
                sum_s[rows, 128:] = jnp.broadcast_to(jnp.sum(gh * gain[...], axis=1, keepdims=True), (16, 128))
        c = partner_copy(sum_s, sum_r)
        gain_s[0] = jnp.sum(gain8[...], axis=0, keepdims=True)
        return c

    def ln_back_last(c):
        c.wait()
        sum_r[...] = (sum_s[...] + sum_r[...]) / 6144.0

        @pl.loop(0, 2)
        def _(p):
            @pl.loop(0, 4)
            def _(t):
                rows = pl.ds(pl.multiple_of(p * 64 + t * 16, 16), 16)
                part = pl.ds(pl.multiple_of(t * 16, 16), 16)
                hat = (x_in[rows, :].astype(F32) - avg[rows, :1]) * inv[rows, :1]
                g = gin_out[p, part, :] * gain[...]
                gin_out[p, part, :] = inv[rows, :1] * (g - sum_r[rows, :1] - hat * sum_r[rows, 128:129])

    def gain_reduce():
        step = 0
        for ax in ("z", "x", "y"):
            i = coord[ax]
            for other in (i + 1 - 2 * (i % 2), 3 - i):
                c = rcopy(gain_s.at[step], gain_r.at[step], alloc(), dev(ax, other))
                c.start()
                yield
                c.wait()
                gain_s[step + 1] = gain_s[step] + gain_r[step]
                step += 1
        gain_out[...] = gain_s[step]
        yield

    outgoing = []

    def leave(src, dst):
        c = pltpu.make_async_copy(src, dst, osem.at[len(outgoing)])
        c.start()
        outgoing.append(c)

    sg = [small_gather(u) for u in range(4)]
    bg = [big_gather(u) for u in range(4)]
    z_cot = ring_gather("z", lambda p, i: cot.at[i, p], 0, 1)
    z_normed = ring_gather("z", lambda p, i: normed.at[i, p], 0, 1)
    units = (1, 2, 3, 0)
    rs = [big_scatter(u, k % 2) for k, u in enumerate(units)]
    ps = [small_scatter(u) for u in units]
    z_gn = ring_scatter("z", lambda p, i: gn.at[i, p], 0, 1, lambda n: zg_buf.at[n], emit_gn)
    z_branch = ring_scatter("z", lambda p, i: bpart.at[i, p], 0, 1, lambda n: zb_buf.at[n], emit_branch)

    for c in local[:4]:
        c.wait()
    next(sg[0])
    local[4].wait()
    next(z_cot)
    for c in local[5:]:
        c.wait()
    next(sg[1])
    idr[r] = ids_row[...]
    ids_a = partner_copy(idr.at[r], idr.at[r])
    stats = ln_stats()
    next(sg[0])
    next(sg[1])
    ln_apply(stats)
    next(sg[0])
    next(bg[0])
    next(sg[2])
    next(z_cot)
    next(z_normed)
    next(sg[1])
    next(bg[0])
    next(sg[2])
    next(bg[1])
    next(z_cot)
    next(bg[0])
    next(sg[3])
    gcopy = gatt_first()
    ids_a.wait()
    id_columns()
    next(z_normed)
    next(sg[2])
    next(bg[1])
    next(sg[3])
    next(bg[2])
    gatt_last(gcopy)
    next(z_normed)
    next(sg[3])
    next(bg[1])

    pc = proj_a(0)
    next(bg[2])
    proj_b(0)
    next(bg[3])
    ex0 = attention(0, pc)
    for e in ex0:
        e.wait()
    weight_grad(0, 0, 8)
    next(bg[2])
    pc = proj_a(1)
    proj_b(1)
    next(bg[3])
    next(rs[0])
    ex1 = attention(1, pc)
    for e in ex1:
        e.wait()
    weight_grad(1, 0, 8)
    next(rs[0])
    next(rs[1])
    next(bg[3])
    pc = proj_a(2)
    proj_b(2)
    ex2 = attention(2, pc)
    next(rs[0])
    release(0)
    next(ps[0])
    ex2[0].wait()
    weight_grad(2, 0, 4)
    next(rs[1])
    next(ps[0])
    weight_grad(2, 4, 8)
    acquire(0)
    next(rs[2])
    next(z_gn)
    ex2[1].wait()
    out_grad()
    next(z_branch)
    next(rs[1])
    release(1)
    next(ps[1])
    next(ps[0])
    acquire(1)
    next(rs[3])
    next(z_gn)
    next(rs[2])
    next(ps[1])
    next(z_gn)
    next(rs[2])
    next(ps[2])
    next(ps[1])
    back = ln_back_first()
    reduce = gain_reduce()
    next(reduce)
    next(z_branch)
    next(rs[3])
    next(ps[2])
    next(reduce)
    ln_back_last(back)
    leave(gin_out, gin_hbm)
    next(reduce)
    next(reduce)
    next(rs[3])
    next(ps[3])
    next(ps[2])
    leave(gqkv_out, gqkv_hbm)
    next(reduce)
    next(ps[3])
    next(reduce)
    next(reduce)
    next(z_branch)
    leave(branch_out, branch_hbm)
    next(ps[3])
    leave(gout_out, gout_hbm)
    for c in outgoing:
        c.wait()


def copy_out(*refs):
    ins, outs, mids, sems = refs[:5], refs[5:10], refs[10:15], refs[15]
    loads = [pltpu.make_async_copy(ins[k], mids[k], sems.at[0, k]) for k in range(5)]
    stores = [pltpu.make_async_copy(mids[k], outs[k], sems.at[1, k]) for k in range(5)]
    for c in loads:
        c.start()
    for load, store in zip(loads, stores):
        load.wait()
        store.start()
    for c in stores:
        c.wait()


def shards(inputs, norm_gain, w_qkv, w_out, segment_ids, cotangent):
    own_ids = segment_ids[0]
    vmem = pl.BlockSpec(memory_space=pltpu.VMEM)
    hbm = pl.BlockSpec(memory_space=pl.ANY)
    V = pltpu.VMEM
    outs = pl.pallas_call(
        kernel,
        out_shape=(
            jax.ShapeDtypeStruct((2, 64, 3072), BF16),
            jax.ShapeDtypeStruct((2, 64, 3072), F32),
            jax.ShapeDtypeStruct((1, 3072), F32),
            jax.ShapeDtypeStruct((4, 48, 2304), F32),
            jax.ShapeDtypeStruct((48, 3072), F32),
        ),
        in_specs=[hbm, vmem, hbm, hbm, vmem, hbm],
        out_specs=(hbm, hbm, vmem, hbm, hbm),
        scratch_shapes=[
            V((128, 3072), BF16),
            V((2, 64, 3072), BF16),
            V((2, 64, 3072), F32),
            V((4, 48, 2304), F32),
            V((48, 3072), F32),
            V((3, 4, 4, 4, 48, 768), BF16),
            V((4, 4, 4, 48, 768), BF16),
            V((2, 12, 4, 48, 768), BF16),
            V((4, 12, 48, 768), BF16),
            V((4, 2, 64, 3072), BF16),
            V((4, 2, 64, 3072), BF16),
            V((4, 2, 64, 3072), BF16),
            V((4, 2, 64, 3072), BF16),
            V((6, 64, 3072), BF16),
            V((6, 64, 3072), BF16),
            V((512, 384), F32),
            V((3, 512, 384), BF16),
            V((3, 512, 384), BF16),
            V((512, 384), BF16),
            V((512, 384), BF16),
            V((512, 384), BF16),
            V((512, 768), BF16),
            V((3, 512, 768), BF16),
            V((512, 128), BF16),
            V((512, 128), BF16),
            V((512, 128), F32),
            V((512, 128), F32),
            V((2, 1, 256), jnp.int32),
            V((4, 128, 128), F32),
            V((128, 256), F32),
            V((128, 256), F32),
            V((128, 128), F32),
            V((128, 128), F32),
            V((128, 256), F32),
            V((128, 256), F32),
            V((8, 3072), F32),
            V((7, 1, 3072), F32),
            V((6, 1, 3072), F32),
            pltpu.SemaphoreType.DMA((N_SEM,)),
            pltpu.SemaphoreType.DMA((N_SEM,)),
            pltpu.SemaphoreType.DMA((12,)),
            pltpu.SemaphoreType.DMA((4,)),
            pltpu.SemaphoreType.REGULAR((2,)),
        ],
        compiler_params=pltpu.CompilerParams(
            collective_id=0, has_side_effects=True, vmem_limit_bytes=62 * 1024 * 1024
        ),
    )(
        inputs,
        norm_gain.reshape(1, 3072),
        w_qkv.reshape(4, 48, 2304),
        w_out,
        own_ids.reshape(1, 256),
        cotangent.reshape(2, 64, 3072),
    )
    branch, gin, gain, gqkv, gout = pl.pallas_call(
        copy_out,
        out_shape=tuple(jax.ShapeDtypeStruct(o.shape, o.dtype) for o in outs),
        in_specs=[hbm] * 5,
        out_specs=(hbm,) * 5,
        scratch_shapes=[V(o.shape, o.dtype) for o in outs] + [pltpu.SemaphoreType.DMA((2, 5))],
    )(*outs)
    return (
        branch.reshape(128, 3072), gin.reshape(128, 3072), gain.reshape(3072),
        gqkv.reshape(192, 2304), gout,
    )


def solution(mesh):
    placed = (
        P(("depth", "col"), "row"),
        P("row"),
        P(("row", "depth"), "col"),
        P(("col", "depth"), "row"),
        P("depth", "row"),
        P(("depth", "col"), "row"),
    )
    return jax.shard_map(
        shards,
        mesh=mesh,
        in_specs=placed,
        out_specs=(
            P(("depth", "col"), "row"),
            P(("depth", "col"), "row"),
            P("row"),
            P(("row", "depth"), "col"),
            P(("col", "depth"), "row"),
        ),
        check_vma=False,
    )
```

```python
import math

import jax
import jax.numpy as jnp
from jax import lax
from jax.experimental import pallas as pl
from jax.experimental.pallas import tpu as pltpu
from jax.sharding import PartitionSpec as P

HD = 128
EPSILON = 1e-06
SCALE = 1.0 / math.sqrt(HD)
F32 = jnp.float32
BF16 = jnp.bfloat16
N_SEM = 240


def mm(a, b, ca=1, cb=0):
    return lax.dot_general(a, b, (((ca,), (cb,)), ((), ())), preferred_element_type=F32)


def norm_parts(v):
    centre = v - jnp.mean(v, axis=-1, keepdims=True)
    rs = lax.rsqrt(jnp.mean(centre * centre, axis=-1, keepdims=True) + EPSILON)
    return centre * rs, rs


def norm_back(hat, rs, g):
    dc = rs * (g - hat * jnp.mean(g * hat, axis=-1, keepdims=True))
    return dc - jnp.mean(dc, axis=-1, keepdims=True)


def kernel(
    x_hbm, gain, w_in, wo_in, ids_row, cot_in,
    branch_hbm, gin_hbm, gain_out, gqkv_hbm, gout_hbm,
    x_in, branch_out, gin_out, gqkv_out, gout_out,
    wq, wo, ra, rbm, pa, pbm, normed, cot, gn, bpart, zb_buf, zg_buf,
    acc, tmp, psend, precv, crecv, gacc, gsend, grecv, gcr, gatt, att, gp,
    khat, vals, dk, dv, idr, idc, stat_s, stat_r, avg, inv, sum_s, sum_r,
    nstage, bstage, gstage, grest, ostage, orecv,
    gain8, gain_s, gain_r,
    ssem, rsem, lsem, osem,
):
    depth = lax.axis_index("depth")
    r = lax.axis_index("row")
    z = lax.axis_index("col")
    y, x = depth // 4, depth % 4
    h, xo = x // 2, x % 2
    coord = {"x": x, "y": y, "z": z}
    counter = [0]

    def alloc():
        counter[0] += 1
        return counter[0] - 1

    def dev(ax, i):
        if ax == "x":
            return {"depth": y * 4 + i}
        if ax == "y":
            return {"depth": i * 4 + x}
        return {"col": i}

    core = {"row": 1 - r}
    pair = {"depth": y * 4 + 3 - x}
    mate = {"depth": y * 4 + x + 1 - 2 * xo}

    def rcopy(src, dst, k, device):
        return pltpu.make_async_remote_copy(
            src_ref=src, dst_ref=dst, send_sem=ssem.at[k], recv_sem=rsem.at[k],
            device_id=device, device_id_type=pl.DeviceIdType.MESH,
        )

    def send(src, dst, device):
        c = rcopy(src, dst, alloc(), device)
        c.start()
        return c

    def nb(ax):
        i = coord[ax]
        return i, lax.rem(i + 1, 4), lax.rem(i + 3, 4), lax.rem(i + 2, 4)

    def lanes(start, size):
        return pl.ds(pl.multiple_of(start, 128), size)

    nbrs = [core, pair, mate]
    for ax in ("y", "z"):
        _, up, dn, _ = nb(ax)
        nbrs += [dev(ax, up), dev(ax, dn)]
    barrier = pltpu.get_barrier_semaphore()
    for d in nbrs:
        pl.semaphore_signal(barrier, inc=1, device_id=d, device_id_type=pl.DeviceIdType.MESH)

    local = []

    def lcopy(src, dst):
        c = pltpu.make_async_copy(src, dst, lsem.at[len(local)])
        c.start()
        local.append(c)

    mine, theirs = h * 1536, (1 - h) * 1536
    lcopy(cot_in.at[:, lanes(mine, 1536)], cot.at[0, z])
    lcopy(x_hbm, x_in)
    for c in range(3):
        lcopy(w_in.at[:, :, pl.ds(c * 384, 384)], wq.at[c, y, xo, :, :, pl.ds(0, 384)])
        lcopy(w_in.at[:, :, pl.ds((3 + c) * 384, 384)], wq.at[c, y, xo, :, :, pl.ds(384, 384)])
    for cb in range(2):
        lcopy(wo_in.at[:, lanes(mine + cb * 768, 768)], wo.at[y, xo, cb])
    pl.semaphore_wait(barrier, len(nbrs))

    def ring_gather(ax, blk, p0, p1, late=False):
        i, up, dn, op = nb(ax)
        to_up, to_dn = dev(ax, up), dev(ax, dn)
        k = [alloc() for _ in range(6)]
        sent = []

        def go(b, kk, device):
            c = rcopy(b, b, kk, device)
            c.start()
            sent.append(c)

        def got(b, kk, device):
            rcopy(b, b, kk, device).wait_recv()

        go(blk(p0, i), k[0], to_up)
        if late:
            go(blk(p0, i), k[3], to_dn)
            yield
        go(blk(p1, i), k[1], to_dn)
        go(blk(p1, i), k[2], to_up)
        if not late:
            go(blk(p0, i), k[3], to_dn)
        yield
        got(blk(p0, dn), k[0], to_up)
        go(blk(p0, dn), k[4], to_up)
        got(blk(p1, up), k[1], to_dn)
        go(blk(p1, up), k[5], to_dn)
        yield
        got(blk(p1, dn), k[2], to_up)
        got(blk(p0, up), k[3], to_dn)
        got(blk(p0, op), k[4], to_up)
        got(blk(p1, op), k[5], to_dn)
        for c in sent:
            c.wait_send()
        yield

    def over(ref, f):
        shape = ref.shape
        if len(shape) == 4:
            @pl.loop(0, shape[0])
            def _(j):
                for k in range(shape[1]):
                    f((j, k))
        elif len(shape) == 3:
            @pl.loop(0, shape[0])
            def _(j):
                f(j)
        else:
            rows = 16

            @pl.loop(0, shape[0] // rows)
            def _(j):
                f(pl.ds(pl.multiple_of(j * rows, rows), rows))

    def add_into(dst, *srcs):
        def f(j):
            total = dst[j].astype(F32)
            for src in srcs:
                total = total + src[j].astype(F32)
            dst[j] = total.astype(BF16)
        over(dst, f)

    def emit_sum(p, own, a, b):
        add_into(own, a, b)

    def ring_scatter(ax, blk, p0, p1, buf, emit, late=False):
        i, up, dn, op = nb(ax)
        to_up, to_dn = dev(ax, up), dev(ax, dn)
        k = [alloc() for _ in range(6)]
        sent = []

        def go(b, n, device):
            c = rcopy(b, buf(n), k[n], device)
            c.start()
            sent.append(c)

        def got(n, device):
            rcopy(buf(n), buf(n), k[n], device).wait_recv()

        go(blk(p0, op), 0, to_up)
        go(blk(p1, op), 1, to_dn)
        if late:
            yield
        go(blk(p1, up), 2, to_up)
        go(blk(p0, dn), 3, to_dn)
        yield
        got(0, to_up)
        add_into(blk(p0, up), buf(0))
        go(blk(p0, up), 4, to_up)
        got(1, to_dn)
        add_into(blk(p1, dn), buf(1))
        go(blk(p1, dn), 5, to_dn)
        yield
        for n, device in ((2, to_up), (3, to_dn), (4, to_up), (5, to_dn)):
            got(n, device)
        emit(p0, blk(p0, i), buf(3), buf(4))
        emit(p1, blk(p1, i), buf(2), buf(5))
        for c in sent:
            c.wait_send()
        yield

    def unit(u):
        return wo if u == 0 else wq.at[u - 1]

    def swap(src, dst):
        c = send(src, dst, mate)
        yield
        yield
        c.wait()
        yield

    def both(a, b):
        for _ in range(3):
            next(a)
            next(b)
            yield

    def small_gather(u):
        w = unit(u)
        block = w.at[y, xo, pl.ds(0, 2)]
        return both(swap(block, block), ring_gather("y", lambda p, i: w.at[i, xo, p], 2, 3))

    def big_gather(u):
        w = unit(u)
        block = w.at[:, xo, pl.ds(2, 2)]
        return both(swap(block, block), ring_gather("y", lambda p, i: w.at[i, :, p], 0, 1))

    def big_scatter(u):
        w = unit(u)

        def column():
            yield from swap_add(w.at[:, 1 - xo, pl.ds(2, 2)], rbm.at[u], w.at[:, xo, pl.ds(2, 2)])
        return both(column(), ring_scatter("y", lambda p, i: w.at[i, :, p], 0, 1, lambda n: ra.at[u, n], emit_sum))

    def swap_add(src, buf, dst):
        c = send(src, buf, mate)
        yield
        yield
        c.wait()
        add_into(dst, buf)
        yield

    def small_scatter(u):
        w = unit(u)

        def place(p, j, total):
            if u == 0 and p < 2:
                gout_out[j, lanes(mine + p * 768, 768)] = total
            elif u == 0:
                ostage[p - 2, j] = total.astype(BF16)
            else:
                c = u - 1
                gqkv_out[p, j, c * 384:(c + 1) * 384] = total[:, :384]
                gqkv_out[p, j, (3 + c) * 384:(4 + c) * 384] = total[:, 384:]

        def emit(p, own, a, b):
            over(own, lambda j: place(p, j, own[j].astype(F32) + a[j].astype(F32) + b[j].astype(F32)))

        def row():
            c = send(w.at[y, 1 - xo, pl.ds(0, 2)], pbm.at[u], mate)
            yield
            yield
            c.wait()
            for p in range(2):
                own = w.at[y, xo, p]
                over(own, lambda j: place(p, j, own[j].astype(F32) + pbm[u, p, j].astype(F32)))
            yield
        return both(row(), ring_scatter("y", lambda p, i: w.at[i, xo, p], 2, 3, lambda n: pa.at[u, n], emit))

    def id_columns():
        for t in range(4):
            row = idr[t // 2][:, (t % 2) * 128:(t % 2 + 1) * 128].astype(F32)
            idc[t] = jnp.transpose(jnp.broadcast_to(row, (128, 128)))

    def ln_stats():
        @pl.loop(0, 4)
        def _(t):
            rows = pl.ds(pl.multiple_of(t * 32, 32), 32)
            v = x_in[rows, :].astype(F32)
            stat_s[rows, :128] = jnp.broadcast_to(jnp.sum(v, axis=1, keepdims=True), (32, 128))
            stat_s[rows, 128:] = jnp.broadcast_to(jnp.sum(v * v, axis=1, keepdims=True), (32, 128))
        return send(stat_s, stat_r, core)

    def ln_apply(copy):
        copy.wait()
        total = stat_s[...] + stat_r[...]
        average = total[:, :128] / 6144.0
        variance = total[:, 128:] / 6144.0 - average * average
        avg[...] = average
        inv[...] = lax.rsqrt(variance + EPSILON)

        def half(which, store):
            @pl.loop(0, 4)
            def _(t):
                rows = pl.ds(pl.multiple_of(t * 32, 32), 32)
                for yy in range(4):
                    cols = lanes(yy * 768 + which * 384, 384)
                    hat = (x_in[rows, cols].astype(F32) - avg[rows, :1]) * inv[rows, :1]
                    store(rows, yy * 384, (hat * gain[:, cols]).astype(BF16))

        def to_pair(rows, at, v):
            nstage[rows, at:at + 384] = v

        def to_own(rows, at, v):
            normed[0, z, rows, at:at + 384] = v

        half(1 - h, to_pair)
        c = send(nstage, normed.at[1, z], pair)
        half(h, to_own)
        return c

    def reduce_out(part, far, own, box_s, box_r, chip_r):
        part(1, 1 - r, far)
        box_s[1] = far[...].astype(BF16)
        a = send(box_s.at[1], box_r.at[1], core)
        part(1, r, far)
        part(0, 1 - r, own)
        box_s[0] = own[...].astype(BF16)
        b = send(box_s.at[0], box_r.at[0], core)
        a.wait()
        box_s[1] = (far[...] + box_r[1].astype(F32)).astype(BF16)
        c = send(box_s.at[1], chip_r, pair)
        part(0, r, own)
        b.wait()
        own[...] += box_r[0].astype(F32)
        return c

    def wo_block(yy, xx, cb):
        if xx < 2:
            return (yy, xx + h * (1 - 2 * xx), 2 * h + cb)
        return (yy, (xx - 2) * h + (3 - xx) * (1 - h), 2 * (1 - h) + cb)

    def gatt_part(slot, who, ref):
        for cb in range(2):
            left = cot[slot, :, :, cb * 768:(cb + 1) * 768].reshape(512, 768)
            right = jnp.concatenate([wo[wo_block(2 * who + k, xx, cb)] for k in range(2) for xx in range(4)], axis=0)
            part = mm(left, right, 1, 1)
            if cb == 0:
                ref[...] = part
            else:
                ref[...] += part

    def gatt_first():
        return reduce_out(gatt_part, tmp, gacc, gsend, grecv, gcr)

    def gatt_last(c):
        c.wait()
        gatt[...] = (gacc[...] + gcr[...].astype(F32)).astype(BF16)

    def proj(c):
        def part(slot, who, ref):
            for k in range(2):
                left = normed[slot, :, :, k * 768:(k + 1) * 768].reshape(512, 768)
                right = wq[c, 2 * k:2 * k + 2, :, :, :, lanes(who * 384, 384)].reshape(768, 384)
                v = mm(left, right)
                if k == 0:
                    ref[...] = v
                else:
                    ref[...] += v
        return reduce_out(part, tmp, acc.at[c], psend.at[c], precv.at[c], crecv.at[c])

    def attention(c):
        a = acc.at[c]
        a[...] += crecv[c].astype(F32)
        hat, _ = norm_parts(a[:, 128:256])
        khat[...] = hat.astype(BF16)
        vals[...] = a[:, 256:].astype(BF16)
        dk[...] = jnp.zeros_like(dk)
        dv[...] = jnp.zeros_like(dv)
        head = lanes((3 * r + c) * 128, 128)
        base = pl.multiple_of(r * 384, 128)

        @pl.loop(0, 4)
        def _(t):
            rows = pl.ds(pl.multiple_of(t * 128, 128), 128)
            qh, rs = norm_parts(a[rows, :128])
            ql = qh.astype(BF16)
            ids = jnp.concatenate([idr[0], idr[1]], axis=1).astype(F32)
            same = idc[t][:, :1] == ids
            weights = jnp.where(same, jnp.exp(mm(ql, khat[...], 1, 1) * SCALE), 0.0)
            probs = weights * (1.0 / jnp.sum(weights, axis=-1, keepdims=True))
            low = probs.astype(BF16)
            out = mm(low, vals[...]).astype(BF16)
            att[0, rows, head] = out
            go = gatt[rows, c * 128:(c + 1) * 128]
            dot = jnp.sum(go.astype(F32) * out.astype(F32), axis=-1, keepdims=True)
            gl = (probs * (mm(go, vals[...], 1, 1) - dot)).astype(BF16)
            dq = mm(gl, khat[...]) * SCALE
            dk[...] += mm(gl, ql, 0, 0)
            dv[...] += mm(low, go, 0, 0)
            gp[c, 0, rows, pl.ds(base, 128)] = norm_back(qh, rs, dq).astype(BF16)

        hat, rs = norm_parts(a[:, 128:256])
        gp[c, 0, :, pl.ds(pl.multiple_of(base + 128, 128), 128)] = norm_back(hat, rs, dk[...] * SCALE).astype(BF16)
        gp[c, 0, :, pl.ds(pl.multiple_of(base + 256, 128), 128)] = dv[...].astype(BF16)
        spots = [(att.at[0, :, head], att.at[1, :, head]), (gp.at[c, 0, :, pl.ds(base, 384)], gp.at[c, 1, :, pl.ds(base, 384)])]
        def move(k):
            near, far = spots[k]
            return send(near, far, pair), far, send(near, near, core)
        return move

    def forward(move):
        chip, far, near = move
        chip.wait_recv()
        return near, chip, send(far, far, core)

    def settle(move):
        for c in (move[0], move[2]):
            c.wait()
        move[1].wait_send()

    def weight_grad(c):
        @pl.loop(0, 4)
        def _(f):
            right = wq[c, f].reshape(384, 768)
            cols = lanes(f * 384, 384)
            both_groups = gp[c].reshape(1024, 768)
            for slot in range(2):
                part = mm(gp[c, slot], right, 1, 1).reshape(4, 128, 384)
                if c > 0:
                    part = part + gn[slot, :, :, cols].astype(F32)
                gn[slot, :, :, cols] = part.astype(BF16)
            left = normed[:, :, :, cols].reshape(1024, 384)
            wq[c, f] = mm(left, both_groups, 0, 0).astype(BF16).reshape(2, 4, 48, 768)

    def out_grad():
        for cb in range(2):
            places = [wo_block(yy, xx, cb) for yy in range(4) for xx in range(4)]

            @pl.loop(0, 2)
            def _(q):
                cols, part = lanes(cb * 768 + q * 384, 384), lanes(q * 384, 384)
                right = jnp.concatenate([wo[(*p, slice(None), part)] for p in places], axis=0)
                for slot in range(2):
                    bpart[slot, :, :, cols] = mm(att[slot], right).astype(BF16).reshape(4, 128, 384)
                heads = att[...].reshape(1024, 768)
                total = mm(heads, cot[:, :, :, cols].reshape(1024, 384), 0, 0).astype(BF16)
                for n, p in enumerate(places):
                    wo[(*p, slice(None), part)] = total[n * 48:(n + 1) * 48]

    def emit_branch(slot, p, own, a, b):
        @pl.loop(0, 4)
        def _(t):
            j = pl.ds(pl.multiple_of(t * 16, 16), 16)
            rows = pl.ds(pl.multiple_of(p * 64 + t * 16, 16), 16)
            total = (own[j].astype(F32) + a[j].astype(F32) + b[j].astype(F32)).astype(BF16)
            if slot == 0:
                branch_out[rows, lanes(mine, 1536)] = total
            else:
                bstage[rows] = total

    def emit_gn(slot, p, own, a, b):
        @pl.loop(0, 4)
        def _(t):
            j = pl.ds(pl.multiple_of(t * 16, 16), 16)
            rows = pl.ds(pl.multiple_of(p * 64 + t * 16, 16), 16)
            total = own[j].astype(F32) + a[j].astype(F32) + b[j].astype(F32)
            if slot == 0:
                for yy in range(4):
                    gin_out[rows, lanes(yy * 768 + h * 384, 384)] = total[:, yy * 384:(yy + 1) * 384]
            else:
                gstage[rows] = total.astype(BF16)

    def gn_rest():
        @pl.loop(0, 8)
        def _(t):
            rows = pl.ds(pl.multiple_of(t * 16, 16), 16)
            for yy in range(4):
                gin_out[rows, lanes(yy * 768 + (1 - h) * 384, 384)] = grest[rows, yy * 384:(yy + 1) * 384].astype(F32)

    def ln_back_first():
        gain8[...] = jnp.zeros_like(gain8)

        @pl.loop(0, 8)
        def _(t):
            rows = pl.ds(pl.multiple_of(t * 16, 16), 16)
            hat = (x_in[rows, :].astype(F32) - avg[rows, :1]) * inv[rows, :1]
            g = gin_out[rows, :]
            gh = g * hat
            gain8[...] += gh.reshape(2, 8, 3072).sum(0)
            sum_s[rows, :128] = jnp.broadcast_to(jnp.sum(g * gain[...], axis=1, keepdims=True), (16, 128))
            sum_s[rows, 128:] = jnp.broadcast_to(jnp.sum(gh * gain[...], axis=1, keepdims=True), (16, 128))
        c = send(sum_s, sum_r, core)
        gain_s[0] = jnp.sum(gain8[...], axis=0, keepdims=True)
        return c

    def ln_back_last(c):
        c.wait()
        sum_r[...] = (sum_s[...] + sum_r[...]) / 6144.0

        @pl.loop(0, 8)
        def _(t):
            rows = pl.ds(pl.multiple_of(t * 16, 16), 16)
            hat = (x_in[rows, :].astype(F32) - avg[rows, :1]) * inv[rows, :1]
            g = gin_out[rows, :] * gain[...]
            gin_out[rows, :] = inv[rows, :1] * (g - sum_r[rows, :1] - hat * sum_r[rows, 128:129])

    def gain_reduce():
        step = 0
        for ax in ("z", "x", "y"):
            i = coord[ax]
            for other in (i + 1 - 2 * (i % 2), 3 - i):
                c = send(gain_s.at[step], gain_r.at[step], dev(ax, other))
                yield
                c.wait()
                gain_s[step + 1] = gain_s[step] + gain_r[step]
                step += 1
        gain_out[...] = gain_s[step]
        yield

    outgoing = []

    def leave(src, dst):
        c = pltpu.make_async_copy(src, dst, osem.at[len(outgoing)])
        c.start()
        outgoing.append(c)

    sg = [small_gather(u) for u in range(4)]
    bg = [big_gather(u) for u in range(4)]
    bs = [big_scatter(u) for u in range(4)]
    ps = [small_scatter(u) for u in range(4)]
    z_cot = ring_gather("z", lambda p, i: cot.at[p, i], 0, 1, late=True)
    z_normed = ring_gather("z", lambda p, i: normed.at[p, i], 0, 1, late=True)
    def z_scatter(array, bufs, slot, emit):
        def half(p):
            return pl.ds(p * 64, 64)
        return ring_scatter(
            "z", lambda p, i: array.at[slot, i, half(p)], 0, 1, lambda n: bufs.at[slot * 6 + n],
            lambda p, own, a, b: emit(slot, p, own, a, b),
        )
    z_gn = [z_scatter(gn, zg_buf, slot, emit_gn) for slot in range(2)]
    z_branch = [z_scatter(bpart, zb_buf, slot, emit_branch) for slot in range(2)]

    wo_sems = [alloc(), alloc()]
    wo_pair = []
    for cb in range(2):
        c = rcopy(wo_in.at[:, lanes(theirs + cb * 768, 768)], wo.at[y, 1 - xo, 2 + cb], wo_sems[cb], pair)
        c.start()
        wo_pair.append(c)
    local[0].wait()
    next(z_cot)
    for c in local[2:8]:
        c.wait()
    next(sg[1])
    local[1].wait()
    idr[r] = ids_row[...]
    ids = send(idr.at[r], idr.at[r], core)
    stats = ln_stats()
    next(sg[2])
    next(sg[1])
    normed_pair = ln_apply(stats)
    next(z_normed)
    next(sg[1])
    next(bg[1])
    next(sg[2])
    for c in local[8:]:
        c.wait()
    for cb in range(2):
        wo_pair[cb].wait_send()
        got = wo.at[y, xo, 2 + cb]
        rcopy(got, got, wo_sems[cb], pair).wait_recv()
    next(sg[0])
    next(bg[1])
    normed_pair.wait()
    next(z_normed)
    cot_pair = send(cot_in.at[:, lanes(theirs, 1536)], cot.at[1, z], pair)
    ids.wait()
    id_columns()
    next(sg[2])
    next(bg[2])
    next(sg[0])
    next(bg[1])
    next(sg[3])
    next(sg[0])
    next(bg[2])
    next(bg[0])
    next(sg[3])
    next(z_normed)
    cot_pair.wait()
    next(z_normed)
    next(z_cot)
    pc0 = proj(0)
    next(bg[2])
    next(bg[0])
    next(sg[3])
    next(bg[3])
    pc1 = proj(1)
    next(z_cot)
    next(bg[0])
    next(z_cot)
    gcopy = gatt_first()
    next(bg[3])
    gatt_last(gcopy)
    next(bg[3])
    pc2 = proj(2)
    pc0.wait()
    move0 = attention(0)
    pc1.wait()
    move1 = attention(1)
    pc2.wait()
    atts = [move0(0), move1(0)]
    move2 = attention(2)
    atts.append(move2(0))
    atts = [forward(m) for m in atts]
    gp0 = move0(1)
    for m in atts:
        settle(m)
    out_grad()
    next(z_branch[1])
    next(z_branch[0])
    next(bs[0])
    gp0 = forward(gp0)
    gp1 = move1(1)
    settle(gp0)
    next(bs[0])
    weight_grad(0)
    next(bs[1])
    gp1 = forward(gp1)
    gp2 = move2(1)
    settle(gp1)
    next(bs[0])
    next(ps[0])
    weight_grad(1)
    next(bs[2])
    next(z_branch[1])
    next(bs[1])
    next(z_branch[0])
    next(ps[0])
    gp2 = forward(gp2)
    settle(gp2)
    weight_grad(2)
    next(z_gn[1])
    next(z_gn[0])
    next(bs[3])
    next(bs[1])
    next(ps[1])
    next(z_branch[1])
    branch_sem = alloc()
    branch_pair = rcopy(bstage, branch_out.at[:, lanes(mine, 1536)], branch_sem, pair)
    branch_pair.start()
    next(z_branch[0])
    next(z_gn[1])
    next(bs[2])
    next(z_gn[0])
    next(ps[0])
    out_pair = send(ostage, orecv, pair)
    next(bs[3])
    next(ps[1])
    next(bs[2])
    next(ps[2])
    branch_pair.wait_send()
    got = branch_out.at[:, lanes(theirs, 1536)]
    rcopy(got, got, branch_sem, pair).wait_recv()
    leave(branch_out, branch_hbm)
    next(z_gn[1])
    gn_pair = send(gstage, grest, pair)
    next(ps[1])
    next(ps[2])
    next(z_gn[0])
    out_pair.wait()
    for cb in range(2):
        gout_out[:, lanes(theirs + cb * 768, 768)] = orecv[cb].astype(F32)
    leave(gout_out, gout_hbm)
    gn_pair.wait()
    gn_rest()
    back = ln_back_first()
    reduce = gain_reduce()
    next(reduce)
    next(bs[3])
    next(ps[3])
    next(reduce)
    ln_back_last(back)
    leave(gin_out, gin_hbm)
    next(reduce)
    next(ps[2])
    next(ps[3])
    next(reduce)
    next(reduce)
    next(ps[3])
    leave(gqkv_out, gqkv_hbm)
    next(reduce)
    next(reduce)
    for c in outgoing:
        c.wait()


def copy_out(*refs):
    ins, outs, mids, sems = refs[:5], refs[5:10], refs[10:15], refs[15]
    loads = [pltpu.make_async_copy(ins[k], mids[k], sems.at[0, k]) for k in range(5)]
    stores = [pltpu.make_async_copy(mids[k], outs[k], sems.at[1, k]) for k in range(5)]
    for c in loads:
        c.start()
    for load, store in zip(loads, stores):
        load.wait()
        store.start()
    for c in stores:
        c.wait()


def shards(inputs, norm_gain, w_qkv, w_out, segment_ids, cotangent):
    own_ids = segment_ids[0]
    vmem = pl.BlockSpec(memory_space=pltpu.VMEM)
    hbm = pl.BlockSpec(memory_space=pl.ANY)
    V = pltpu.VMEM
    outs = pl.pallas_call(
        kernel,
        out_shape=(
            jax.ShapeDtypeStruct((128, 3072), BF16),
            jax.ShapeDtypeStruct((128, 3072), F32),
            jax.ShapeDtypeStruct((1, 3072), F32),
            jax.ShapeDtypeStruct((4, 48, 2304), F32),
            jax.ShapeDtypeStruct((48, 3072), F32),
        ),
        in_specs=[hbm, vmem, hbm, hbm, vmem, hbm],
        out_specs=(hbm, hbm, vmem, hbm, hbm),
        scratch_shapes=[
            V((128, 3072), BF16),
            V((128, 3072), BF16),
            V((128, 3072), F32),
            V((4, 48, 2304), F32),
            V((48, 3072), F32),
            V((3, 4, 2, 4, 48, 768), BF16),
            V((4, 2, 4, 48, 768), BF16),
            V((4, 6, 2, 48, 768), BF16),
            V((4, 4, 2, 48, 768), BF16),
            V((4, 6, 48, 768), BF16),
            V((4, 2, 48, 768), BF16),
            V((2, 4, 128, 1536), BF16),
            V((2, 4, 128, 1536), BF16),
            V((2, 4, 128, 1536), BF16),
            V((2, 4, 128, 1536), BF16),
            V((12, 64, 1536), BF16),
            V((12, 64, 1536), BF16),
            V((3, 512, 384), F32),
            V((512, 384), F32),
            V((3, 2, 512, 384), BF16),
            V((3, 2, 512, 384), BF16),
            V((3, 512, 384), BF16),
            V((512, 384), F32),
            V((2, 512, 384), BF16),
            V((2, 512, 384), BF16),
            V((512, 384), BF16),
            V((512, 384), BF16),
            V((2, 512, 768), BF16),
            V((3, 2, 512, 768), BF16),
            V((512, 128), BF16),
            V((512, 128), BF16),
            V((512, 128), F32),
            V((512, 128), F32),
            V((2, 1, 256), jnp.int32),
            V((4, 128, 128), F32),
            V((128, 256), F32),
            V((128, 256), F32),
            V((128, 128), F32),
            V((128, 128), F32),
            V((128, 256), F32),
            V((128, 256), F32),
            V((128, 1536), BF16),
            V((128, 1536), BF16),
            V((128, 1536), BF16),
            V((128, 1536), BF16),
            V((2, 48, 768), BF16),
            V((2, 48, 768), BF16),
            V((8, 3072), F32),
            V((7, 1, 3072), F32),
            V((6, 1, 3072), F32),
            pltpu.SemaphoreType.DMA((N_SEM,)),
            pltpu.SemaphoreType.DMA((N_SEM,)),
            pltpu.SemaphoreType.DMA((10,)),
            pltpu.SemaphoreType.DMA((4,)),
        ],
        compiler_params=pltpu.CompilerParams(
            collective_id=0, has_side_effects=True, vmem_limit_bytes=62 * 1024 * 1024
        ),
    )(
        inputs,
        norm_gain.reshape(1, 3072),
        w_qkv.reshape(4, 48, 2304),
        w_out,
        own_ids.reshape(1, 256),
        cotangent,
    )
    branch, gin, gain, gqkv, gout = pl.pallas_call(
        copy_out,
        out_shape=tuple(jax.ShapeDtypeStruct(o.shape, o.dtype) for o in outs),
        in_specs=[hbm] * 5,
        out_specs=(hbm,) * 5,
        scratch_shapes=[V(o.shape, o.dtype) for o in outs] + [pltpu.SemaphoreType.DMA((2, 5))],
    )(*outs)
    return (
        branch, gin, gain.reshape(3072),
        gqkv.reshape(192, 2304), gout,
    )


def solution(mesh):
    placed = (
        P(("depth", "col"), "row"),
        P("row"),
        P(("row", "depth"), "col"),
        P(("col", "depth"), "row"),
        P("depth", "row"),
        P(("depth", "col"), "row"),
    )
    return jax.shard_map(
        shards,
        mesh=mesh,
        in_specs=placed,
        out_specs=(
            P(("depth", "col"), "row"),
            P(("depth", "col"), "row"),
            P("row"),
            P(("row", "depth"), "col"),
            P(("col", "depth"), "row"),
        ),
        check_vma=False,
    )
```

```python
import math

import jax
import jax.numpy as jnp
from jax import lax
from jax.experimental import pallas as pl
from jax.experimental.pallas import tpu as pltpu
from jax.sharding import PartitionSpec as P

HD = 128
EPSILON = 1e-06
SCALE = 1.0 / math.sqrt(HD)
F32 = jnp.float32
BF16 = jnp.bfloat16
N_SEM = 240


def mm(a, b, ca=1, cb=0):
    return lax.dot_general(a, b, (((ca,), (cb,)), ((), ())), preferred_element_type=F32)


def norm_parts(v):
    centre = v - jnp.mean(v, axis=-1, keepdims=True)
    rs = lax.rsqrt(jnp.mean(centre * centre, axis=-1, keepdims=True) + EPSILON)
    return centre * rs, rs


def norm_back(hat, rs, g):
    dc = rs * (g - hat * jnp.mean(g * hat, axis=-1, keepdims=True))
    return dc - jnp.mean(dc, axis=-1, keepdims=True)


def kernel(
    x_hbm, gain, w_in, wo_in, ids_row, cot_in,
    branch_hbm, gin_hbm, gain_out, gqkv_hbm, gout_hbm,
    x_in, branch_out, gin_out, gqkv_out, gout_out,
    wq, wo, ra, rbm, pa, pbm, normed, cot, gn, bpart, zb_buf, zg_buf,
    acc, tmp, psend, precv, crecv, gacc, gsend, grecv, gcr, gatt, att, gp,
    khat, vals, dk, dv, idr, idc, stat_s, stat_r, avg, inv, sum_s, sum_r,
    nstage, bstage, gstage, grest, ostage, orecv,
    gain8, gain_s, gain_r,
    ssem, rsem, lsem, osem,
):
    depth = lax.axis_index("depth")
    r = lax.axis_index("row")
    z = lax.axis_index("col")
    y, x = depth // 4, depth % 4
    h, xo = x // 2, x % 2
    coord = {"x": x, "y": y, "z": z}
    counter = [0]

    def alloc():
        counter[0] += 1
        return counter[0] - 1

    def dev(ax, i):
        if ax == "x":
            return {"depth": y * 4 + i}
        if ax == "y":
            return {"depth": i * 4 + x}
        return {"col": i}

    core = {"row": 1 - r}
    pair = {"depth": y * 4 + 3 - x}
    mate = {"depth": y * 4 + x + 1 - 2 * xo}

    def rcopy(src, dst, k, device):
        return pltpu.make_async_remote_copy(
            src_ref=src, dst_ref=dst, send_sem=ssem.at[k], recv_sem=rsem.at[k],
            device_id=device, device_id_type=pl.DeviceIdType.MESH,
        )

    def send(src, dst, device):
        c = rcopy(src, dst, alloc(), device)
        c.start()
        return c

    def nb(ax):
        i = coord[ax]
        return i, lax.rem(i + 1, 4), lax.rem(i + 3, 4), lax.rem(i + 2, 4)

    def lanes(start, size):
        return pl.ds(pl.multiple_of(start, 128), size)

    nbrs = [core, pair, mate]
    for ax in ("y", "z"):
        _, up, dn, _ = nb(ax)
        nbrs += [dev(ax, up), dev(ax, dn)]
    nbrs += [dev(ax, nb(ax)[3]) for ax in ("x", "y", "z")]
    barrier = pltpu.get_barrier_semaphore()
    for d in nbrs:
        pl.semaphore_signal(barrier, inc=1, device_id=d, device_id_type=pl.DeviceIdType.MESH)

    local = []

    def lcopy(src, dst):
        c = pltpu.make_async_copy(src, dst, lsem.at[len(local)])
        c.start()
        local.append(c)

    mine, theirs = h * 1536, (1 - h) * 1536
    lcopy(cot_in.at[:, lanes(mine, 1536)], cot.at[0, z])
    lcopy(x_hbm, x_in)
    for c in range(3):
        lcopy(w_in.at[:, :, pl.ds(c * 384, 384)], wq.at[c, y, xo, :, :, pl.ds(0, 384)])
        lcopy(w_in.at[:, :, pl.ds((3 + c) * 384, 384)], wq.at[c, y, xo, :, :, pl.ds(384, 384)])
    for cb in range(2):
        lcopy(wo_in.at[:, lanes(mine + cb * 768, 768)], wo.at[y, xo, cb])
    pl.semaphore_wait(barrier, len(nbrs))

    def ring_gather(ax, blk, p0, p1, late=False):
        i, up, dn, op = nb(ax)
        to_up, to_dn = dev(ax, up), dev(ax, dn)
        k = [alloc() for _ in range(6)]
        sent = []

        def go(b, kk, device):
            c = rcopy(b, b, kk, device)
            c.start()
            sent.append(c)

        def got(b, kk, device):
            rcopy(b, b, kk, device).wait_recv()

        go(blk(p0, i), k[0], to_up)
        if late:
            go(blk(p0, i), k[3], to_dn)
            yield
        go(blk(p1, i), k[1], to_dn)
        go(blk(p1, i), k[2], to_up)
        if not late:
            go(blk(p0, i), k[3], to_dn)
        yield
        got(blk(p0, dn), k[0], to_up)
        go(blk(p0, dn), k[4], to_up)
        got(blk(p1, up), k[1], to_dn)
        go(blk(p1, up), k[5], to_dn)
        yield
        got(blk(p1, dn), k[2], to_up)
        got(blk(p0, up), k[3], to_dn)
        got(blk(p0, op), k[4], to_up)
        got(blk(p1, op), k[5], to_dn)
        for c in sent:
            c.wait_send()
        yield

    def over(ref, f):
        shape = ref.shape
        if len(shape) == 4:
            @pl.loop(0, shape[0])
            def _(j):
                for k in range(shape[1]):
                    f((j, k))
        elif len(shape) == 3:
            @pl.loop(0, shape[0])
            def _(j):
                f(j)
        else:
            rows = 16

            @pl.loop(0, shape[0] // rows)
            def _(j):
                f(pl.ds(pl.multiple_of(j * rows, rows), rows))

    def add_into(dst, *srcs):
        def f(j):
            total = dst[j].astype(F32)
            for src in srcs:
                total = total + src[j].astype(F32)
            dst[j] = total.astype(BF16)
        over(dst, f)

    def emit_sum(p, own, a, b):
        add_into(own, a, b)

    def ring_scatter(ax, blk, p0, p1, buf, emit, late=False):
        i, up, dn, op = nb(ax)
        to_up, to_dn = dev(ax, up), dev(ax, dn)
        k = [alloc() for _ in range(6)]
        sent = []

        def go(b, n, device):
            c = rcopy(b, buf(n), k[n], device)
            c.start()
            sent.append(c)

        def got(n, device):
            rcopy(buf(n), buf(n), k[n], device).wait_recv()

        go(blk(p0, op), 0, to_up)
        go(blk(p1, op), 1, to_dn)
        if late:
            yield
        go(blk(p1, up), 2, to_up)
        go(blk(p0, dn), 3, to_dn)
        yield
        got(0, to_up)
        add_into(blk(p0, up), buf(0))
        go(blk(p0, up), 4, to_up)
        got(1, to_dn)
        add_into(blk(p1, dn), buf(1))
        go(blk(p1, dn), 5, to_dn)
        yield
        for n, device in ((2, to_up), (3, to_dn), (4, to_up), (5, to_dn)):
            got(n, device)
        emit(p0, blk(p0, i), buf(3), buf(4))
        emit(p1, blk(p1, i), buf(2), buf(5))
        for c in sent:
            c.wait_send()
        yield

    def unit(u):
        return wo if u == 0 else wq.at[u - 1]

    def swap(src, dst):
        c = send(src, dst, mate)
        yield
        yield
        c.wait()
        yield

    def both(a, b):
        for _ in range(3):
            next(a)
            next(b)
            yield

    def small_gather(u):
        w = unit(u)
        block = w.at[y, xo, pl.ds(0, 2)]
        return both(swap(block, block), ring_gather("y", lambda p, i: w.at[i, xo, p], 2, 3))

    def big_gather(u):
        w = unit(u)
        block = w.at[:, xo, pl.ds(2, 2)]
        return both(swap(block, block), ring_gather("y", lambda p, i: w.at[i, :, p], 0, 1))

    def big_scatter(u):
        w = unit(u)

        def column():
            yield from swap_add(w.at[:, 1 - xo, pl.ds(2, 2)], rbm.at[u], w.at[:, xo, pl.ds(2, 2)])
        return both(column(), ring_scatter("y", lambda p, i: w.at[i, :, p], 0, 1, lambda n: ra.at[u, n], emit_sum))

    def swap_add(src, buf, dst):
        c = send(src, buf, mate)
        yield
        yield
        c.wait()
        add_into(dst, buf)
        yield

    def small_scatter(u):
        w = unit(u)

        def place(p, j, total):
            if u == 0 and p < 2:
                gout_out[j, lanes(mine + p * 768, 768)] = total
            elif u == 0:
                ostage[p - 2, j] = total.astype(BF16)
            else:
                c = u - 1
                gqkv_out[p, j, c * 384:(c + 1) * 384] = total[:, :384]
                gqkv_out[p, j, (3 + c) * 384:(4 + c) * 384] = total[:, 384:]

        def emit(p, own, a, b):
            over(own, lambda j: place(p, j, own[j].astype(F32) + a[j].astype(F32) + b[j].astype(F32)))

        def row():
            c = send(w.at[y, 1 - xo, pl.ds(0, 2)], pbm.at[u], mate)
            yield
            yield
            c.wait()
            for p in range(2):
                own = w.at[y, xo, p]
                over(own, lambda j: place(p, j, own[j].astype(F32) + pbm[u, p, j].astype(F32)))
            yield
        return both(row(), ring_scatter("y", lambda p, i: w.at[i, xo, p], 2, 3, lambda n: pa.at[u, n], emit))

    def id_columns():
        for t in range(4):
            row = idr[t // 2][:, (t % 2) * 128:(t % 2 + 1) * 128].astype(F32)
            idc[t] = jnp.transpose(jnp.broadcast_to(row, (128, 128)))

    def ln_stats():
        @pl.loop(0, 4)
        def _(t):
            rows = pl.ds(pl.multiple_of(t * 32, 32), 32)
            v = x_in[rows, :].astype(F32)
            stat_s[rows, :128] = jnp.broadcast_to(jnp.sum(v, axis=1, keepdims=True), (32, 128))
            stat_s[rows, 128:] = jnp.broadcast_to(jnp.sum(v * v, axis=1, keepdims=True), (32, 128))
        return send(stat_s, stat_r, core)

    def ln_apply(copy):
        copy.wait()
        total = stat_s[...] + stat_r[...]
        average = total[:, :128] / 6144.0
        variance = total[:, 128:] / 6144.0 - average * average
        avg[...] = average
        inv[...] = lax.rsqrt(variance + EPSILON)

        def half(which, store):
            @pl.loop(0, 4)
            def _(t):
                rows = pl.ds(pl.multiple_of(t * 32, 32), 32)
                for yy in range(4):
                    cols = lanes(yy * 768 + which * 384, 384)
                    hat = (x_in[rows, cols].astype(F32) - avg[rows, :1]) * inv[rows, :1]
                    store(rows, yy * 384, (hat * gain[:, cols]).astype(BF16))

        def to_pair(rows, at, v):
            nstage[rows, at:at + 384] = v

        def to_own(rows, at, v):
            normed[0, z, rows, at:at + 384] = v

        half(1 - h, to_pair)
        c = send(nstage, normed.at[1, z], pair)
        half(h, to_own)
        return c

    def reduce_out(part, far, own, box_s, box_r, chip_r):
        part(1, 1 - r, far)
        box_s[1] = far[...].astype(BF16)
        a = send(box_s.at[1], box_r.at[1], core)
        part(1, r, far)
        part(0, 1 - r, own)
        box_s[0] = own[...].astype(BF16)
        b = send(box_s.at[0], box_r.at[0], core)
        a.wait()
        box_s[1] = (far[...] + box_r[1].astype(F32)).astype(BF16)
        c = send(box_s.at[1], chip_r, pair)
        part(0, r, own)
        b.wait()
        own[...] += box_r[0].astype(F32)
        return c

    def wo_block(yy, xx, cb):
        if xx < 2:
            return (yy, xx + h * (1 - 2 * xx), 2 * h + cb)
        return (yy, (xx - 2) * h + (3 - xx) * (1 - h), 2 * (1 - h) + cb)

    def gatt_part(slot, who, ref):
        for cb in range(2):
            left = cot[slot, :, :, cb * 768:(cb + 1) * 768].reshape(512, 768)
            right = jnp.concatenate([wo[wo_block(2 * who + k, xx, cb)] for k in range(2) for xx in range(4)], axis=0)
            part = mm(left, right, 1, 1)
            if cb == 0:
                ref[...] = part
            else:
                ref[...] += part

    def gatt_first():
        return reduce_out(gatt_part, tmp, gacc, gsend, grecv, gcr)

    def gatt_last(c):
        c.wait()
        gatt[...] = (gacc[...] + gcr[...].astype(F32)).astype(BF16)

    def proj(c):
        def part(slot, who, ref):
            for k in range(2):
                left = normed[slot, :, :, k * 768:(k + 1) * 768].reshape(512, 768)
                right = wq[c, 2 * k:2 * k + 2, :, :, :, lanes(who * 384, 384)].reshape(768, 384)
                v = mm(left, right)
                if k == 0:
                    ref[...] = v
                else:
                    ref[...] += v
        return reduce_out(part, tmp, acc.at[c], psend.at[c], precv.at[c], crecv.at[c])

    def attention(c):
        a = acc.at[c]
        a[...] += crecv[c].astype(F32)
        hat, _ = norm_parts(a[:, 128:256])
        khat[...] = hat.astype(BF16)
        vals[...] = a[:, 256:].astype(BF16)
        dk[...] = jnp.zeros_like(dk)
        dv[...] = jnp.zeros_like(dv)
        head = lanes((3 * r + c) * 128, 128)
        base = pl.multiple_of(r * 384, 128)

        @pl.loop(0, 4)
        def _(t):
            rows = pl.ds(pl.multiple_of(t * 128, 128), 128)
            qh, rs = norm_parts(a[rows, :128])
            ql = qh.astype(BF16)
            ids = jnp.concatenate([idr[0], idr[1]], axis=1).astype(F32)
            same = idc[t][:, :1] == ids
            weights = jnp.where(same, jnp.exp(mm(ql, khat[...], 1, 1) * SCALE), 0.0)
            probs = weights * (1.0 / jnp.sum(weights, axis=-1, keepdims=True))
            low = probs.astype(BF16)
            out = mm(low, vals[...]).astype(BF16)
            att[0, rows, head] = out
            go = gatt[rows, c * 128:(c + 1) * 128]
            dot = jnp.sum(go.astype(F32) * out.astype(F32), axis=-1, keepdims=True)
            gl = (probs * (mm(go, vals[...], 1, 1) - dot)).astype(BF16)
            dq = mm(gl, khat[...]) * SCALE
            dk[...] += mm(gl, ql, 0, 0)
            dv[...] += mm(low, go, 0, 0)
            gp[c, 0, rows, pl.ds(base, 128)] = norm_back(qh, rs, dq).astype(BF16)

        hat, rs = norm_parts(a[:, 128:256])
        gp[c, 0, :, pl.ds(pl.multiple_of(base + 128, 128), 128)] = norm_back(hat, rs, dk[...] * SCALE).astype(BF16)
        gp[c, 0, :, pl.ds(pl.multiple_of(base + 256, 128), 128)] = dv[...].astype(BF16)
        spots = [(att.at[0, :, head], att.at[1, :, head]), (gp.at[c, 0, :, pl.ds(base, 384)], gp.at[c, 1, :, pl.ds(base, 384)])]
        def move(k):
            near, far = spots[k]
            return send(near, far, pair), far, send(near, near, core)
        return move

    def forward(move):
        chip, far, near = move
        chip.wait_recv()
        return near, chip, send(far, far, core)

    def settle(move):
        for c in (move[0], move[2]):
            c.wait()
        move[1].wait_send()

    def weight_grad(c):
        @pl.loop(0, 4)
        def _(f):
            right = wq[c, f].reshape(384, 768)
            cols = lanes(f * 384, 384)
            both_groups = gp[c].reshape(1024, 768)
            for slot in range(2):
                part = mm(gp[c, slot], right, 1, 1).reshape(4, 128, 384)
                if c > 0:
                    part = part + gn[slot, :, :, cols].astype(F32)
                gn[slot, :, :, cols] = part.astype(BF16)
            left = normed[:, :, :, cols].reshape(1024, 384)
            wq[c, f] = mm(left, both_groups, 0, 0).astype(BF16).reshape(2, 4, 48, 768)

    def out_grad():
        for cb in range(2):
            places = [wo_block(yy, xx, cb) for yy in range(4) for xx in range(4)]

            @pl.loop(0, 2)
            def _(q):
                cols, part = lanes(cb * 768 + q * 384, 384), lanes(q * 384, 384)
                right = jnp.concatenate([wo[(*p, slice(None), part)] for p in places], axis=0)
                for slot in range(2):
                    bpart[slot, :, :, cols] = mm(att[slot], right).astype(BF16).reshape(4, 128, 384)
                heads = att[...].reshape(1024, 768)
                total = mm(heads, cot[:, :, :, cols].reshape(1024, 384), 0, 0).astype(BF16)
                for n, p in enumerate(places):
                    wo[(*p, slice(None), part)] = total[n * 48:(n + 1) * 48]

    def emit_branch(slot, p, own, a, b):
        @pl.loop(0, 4)
        def _(t):
            j = pl.ds(pl.multiple_of(t * 16, 16), 16)
            rows = pl.ds(pl.multiple_of(p * 64 + t * 16, 16), 16)
            total = (own[j].astype(F32) + a[j].astype(F32) + b[j].astype(F32)).astype(BF16)
            if slot == 0:
                branch_out[rows, lanes(mine, 1536)] = total
            else:
                bstage[rows] = total

    def emit_gn(slot, p, own, a, b):
        @pl.loop(0, 4)
        def _(t):
            j = pl.ds(pl.multiple_of(t * 16, 16), 16)
            rows = pl.ds(pl.multiple_of(p * 64 + t * 16, 16), 16)
            total = own[j].astype(F32) + a[j].astype(F32) + b[j].astype(F32)
            if slot == 0:
                for yy in range(4):
                    gin_out[rows, lanes(yy * 768 + h * 384, 384)] = total[:, yy * 384:(yy + 1) * 384]
            else:
                gstage[rows] = total.astype(BF16)

    def gn_rest():
        @pl.loop(0, 8)
        def _(t):
            rows = pl.ds(pl.multiple_of(t * 16, 16), 16)
            for yy in range(4):
                gin_out[rows, lanes(yy * 768 + (1 - h) * 384, 384)] = grest[rows, yy * 384:(yy + 1) * 384].astype(F32)

    def ln_back_first():
        gain8[...] = jnp.zeros_like(gain8)

        @pl.loop(0, 8)
        def _(t):
            rows = pl.ds(pl.multiple_of(t * 16, 16), 16)
            hat = (x_in[rows, :].astype(F32) - avg[rows, :1]) * inv[rows, :1]
            g = gin_out[rows, :]
            gh = g * hat
            gain8[...] += gh.reshape(2, 8, 3072).sum(0)
            sum_s[rows, :128] = jnp.broadcast_to(jnp.sum(g * gain[...], axis=1, keepdims=True), (16, 128))
            sum_s[rows, 128:] = jnp.broadcast_to(jnp.sum(gh * gain[...], axis=1, keepdims=True), (16, 128))
        c = send(sum_s, sum_r, core)
        gain_s[0] = jnp.sum(gain8[...], axis=0, keepdims=True)
        return c

    def ln_back_last(c):
        c.wait()
        sum_r[...] = (sum_s[...] + sum_r[...]) / 6144.0

        @pl.loop(0, 8)
        def _(t):
            rows = pl.ds(pl.multiple_of(t * 16, 16), 16)
            hat = (x_in[rows, :].astype(F32) - avg[rows, :1]) * inv[rows, :1]
            g = gin_out[rows, :] * gain[...]
            gin_out[rows, :] = inv[rows, :1] * (g - sum_r[rows, :1] - hat * sum_r[rows, 128:129])

    def gain_reduce():
        for step, ax in enumerate(("z", "x", "y")):
            i, up, dn, op = nb(ax)
            gain_r[step, i] = gain_s[step]
            copies = []
            for k, other in ((alloc(), op), (alloc(), up), (alloc(), dn)):
                c = rcopy(gain_s.at[step], gain_r.at[step, i], k, dev(ax, other))
                c.start()
                copies.append((c, k))
            yield
            for (c, k), source in zip(copies, (op, dn, up)):
                c.wait_send()
                got = gain_r.at[step, source]
                rcopy(got, got, k, dev(ax, source)).wait_recv()
            gain_s[step + 1] = (gain_r[step, 0] + gain_r[step, 1]) + (gain_r[step, 2] + gain_r[step, 3])
        gain_out[...] = gain_s[3]
        yield

    outgoing = []

    def leave(src, dst):
        c = pltpu.make_async_copy(src, dst, osem.at[len(outgoing)])
        c.start()
        outgoing.append(c)

    sg = [small_gather(u) for u in range(4)]
    bg = [big_gather(u) for u in range(4)]
    bs = [big_scatter(u) for u in range(4)]
    ps = [small_scatter(u) for u in range(4)]
    z_cot = ring_gather("z", lambda p, i: cot.at[p, i], 0, 1, late=True)
    z_normed = ring_gather("z", lambda p, i: normed.at[p, i], 0, 1, late=True)
    def z_scatter(array, bufs, slot, emit):
        def half(p):
            return pl.ds(p * 64, 64)
        return ring_scatter(
            "z", lambda p, i: array.at[slot, i, half(p)], 0, 1, lambda n: bufs.at[slot * 6 + n],
            lambda p, own, a, b: emit(slot, p, own, a, b),
        )
    z_gn = [z_scatter(gn, zg_buf, slot, emit_gn) for slot in range(2)]
    z_branch = [z_scatter(bpart, zb_buf, slot, emit_branch) for slot in range(2)]

    wo_sems = [alloc(), alloc()]
    wo_pair = []
    for cb in range(2):
        c = rcopy(wo_in.at[:, lanes(theirs + cb * 768, 768)], wo.at[y, 1 - xo, 2 + cb], wo_sems[cb], pair)
        c.start()
        wo_pair.append(c)
    local[0].wait()
    next(z_cot)
    for c in local[2:8]:
        c.wait()
    next(sg[1])
    local[1].wait()
    idr[r] = ids_row[...]
    ids = send(idr.at[r], idr.at[r], core)
    stats = ln_stats()
    next(sg[2])
    next(sg[1])
    normed_pair = ln_apply(stats)
    next(z_normed)
    next(sg[1])
    next(bg[1])
    next(sg[2])
    for c in local[8:]:
        c.wait()
    for cb in range(2):
        wo_pair[cb].wait_send()
        got = wo.at[y, xo, 2 + cb]
        rcopy(got, got, wo_sems[cb], pair).wait_recv()
    next(sg[0])
    next(bg[1])
    normed_pair.wait()
    next(z_normed)
    cot_pair = send(cot_in.at[:, lanes(theirs, 1536)], cot.at[1, z], pair)
    ids.wait()
    id_columns()
    next(sg[2])
    next(bg[2])
    next(sg[0])
    next(bg[1])
    next(sg[3])
    next(sg[0])
    next(bg[2])
    next(bg[0])
    next(sg[3])
    next(z_normed)
    cot_pair.wait()
    next(z_normed)
    next(z_cot)
    pc0 = proj(0)
    next(bg[2])
    next(bg[0])
    next(sg[3])
    next(bg[3])
    pc1 = proj(1)
    next(z_cot)
    next(bg[0])
    next(z_cot)
    gcopy = gatt_first()
    next(bg[3])
    gatt_last(gcopy)
    next(bg[3])
    pc2 = proj(2)
    pc0.wait()
    move0 = attention(0)
    pc1.wait()
    move1 = attention(1)
    pc2.wait()
    atts = [move0(0), move1(0)]
    move2 = attention(2)
    atts.append(move2(0))
    atts = [forward(m) for m in atts]
    gp0 = move0(1)
    for m in atts:
        settle(m)
    out_grad()
    next(z_branch[1])
    next(z_branch[0])
    next(bs[0])
    gp0 = forward(gp0)
    gp1 = move1(1)
    settle(gp0)
    next(bs[0])
    weight_grad(0)
    next(bs[1])
    gp1 = forward(gp1)
    gp2 = move2(1)
    settle(gp1)
    next(bs[0])
    next(ps[0])
    weight_grad(1)
    next(bs[2])
    next(z_branch[1])
    next(bs[1])
    next(z_branch[0])
    next(ps[0])
    gp2 = forward(gp2)
    settle(gp2)
    weight_grad(2)
    next(z_gn[1])
    next(z_gn[0])
    next(bs[3])
    next(bs[1])
    next(ps[1])
    next(z_branch[1])
    branch_sem = alloc()
    branch_pair = rcopy(bstage, branch_out.at[:, lanes(mine, 1536)], branch_sem, pair)
    branch_pair.start()
    next(z_branch[0])
    next(z_gn[1])
    next(bs[2])
    next(z_gn[0])
    next(ps[0])
    out_pair = send(ostage, orecv, pair)
    next(bs[3])
    next(ps[1])
    next(bs[2])
    next(ps[2])
    branch_pair.wait_send()
    got = branch_out.at[:, lanes(theirs, 1536)]
    rcopy(got, got, branch_sem, pair).wait_recv()
    leave(branch_out, branch_hbm)
    next(z_gn[1])
    gn_pair = send(gstage, grest, pair)
    next(ps[1])
    next(ps[2])
    next(z_gn[0])
    out_pair.wait()
    for cb in range(2):
        gout_out[:, lanes(theirs + cb * 768, 768)] = orecv[cb].astype(F32)
    leave(gout_out, gout_hbm)
    gn_pair.wait()
    gn_rest()
    back = ln_back_first()
    reduce = gain_reduce()
    next(reduce)
    next(bs[3])
    next(ps[3])
    next(reduce)
    ln_back_last(back)
    leave(gin_out, gin_hbm)
    next(reduce)
    next(ps[2])
    next(ps[3])
    next(reduce)
    next(ps[3])
    leave(gqkv_out, gqkv_hbm)
    for c in outgoing:
        c.wait()


def copy_out(*refs):
    ins, outs, mids, sems = refs[:5], refs[5:10], refs[10:15], refs[15]
    loads = [pltpu.make_async_copy(ins[k], mids[k], sems.at[0, k]) for k in range(5)]
    stores = [pltpu.make_async_copy(mids[k], outs[k], sems.at[1, k]) for k in range(5)]
    for c in loads:
        c.start()
    for load, store in zip(loads, stores):
        load.wait()
        store.start()
    for c in stores:
        c.wait()


def shards(inputs, norm_gain, w_qkv, w_out, segment_ids, cotangent):
    own_ids = segment_ids[0]
    vmem = pl.BlockSpec(memory_space=pltpu.VMEM)
    hbm = pl.BlockSpec(memory_space=pl.ANY)
    V = pltpu.VMEM
    outs = pl.pallas_call(
        kernel,
        out_shape=(
            jax.ShapeDtypeStruct((128, 3072), BF16),
            jax.ShapeDtypeStruct((128, 3072), F32),
            jax.ShapeDtypeStruct((1, 3072), F32),
            jax.ShapeDtypeStruct((4, 48, 2304), F32),
            jax.ShapeDtypeStruct((48, 3072), F32),
        ),
        in_specs=[hbm, vmem, hbm, hbm, vmem, hbm],
        out_specs=(hbm, hbm, vmem, hbm, hbm),
        scratch_shapes=[
            V((128, 3072), BF16),
            V((128, 3072), BF16),
            V((128, 3072), F32),
            V((4, 48, 2304), F32),
            V((48, 3072), F32),
            V((3, 4, 2, 4, 48, 768), BF16),
            V((4, 2, 4, 48, 768), BF16),
            V((4, 6, 2, 48, 768), BF16),
            V((4, 4, 2, 48, 768), BF16),
            V((4, 6, 48, 768), BF16),
            V((4, 2, 48, 768), BF16),
            V((2, 4, 128, 1536), BF16),
            V((2, 4, 128, 1536), BF16),
            V((2, 4, 128, 1536), BF16),
            V((2, 4, 128, 1536), BF16),
            V((12, 64, 1536), BF16),
            V((12, 64, 1536), BF16),
            V((3, 512, 384), F32),
            V((512, 384), F32),
            V((3, 2, 512, 384), BF16),
            V((3, 2, 512, 384), BF16),
            V((3, 512, 384), BF16),
            V((512, 384), F32),
            V((2, 512, 384), BF16),
            V((2, 512, 384), BF16),
            V((512, 384), BF16),
            V((512, 384), BF16),
            V((2, 512, 768), BF16),
            V((3, 2, 512, 768), BF16),
            V((512, 128), BF16),
            V((512, 128), BF16),
            V((512, 128), F32),
            V((512, 128), F32),
            V((2, 1, 256), jnp.int32),
            V((4, 128, 128), F32),
            V((128, 256), F32),
            V((128, 256), F32),
            V((128, 128), F32),
            V((128, 128), F32),
            V((128, 256), F32),
            V((128, 256), F32),
            V((128, 1536), BF16),
            V((128, 1536), BF16),
            V((128, 1536), BF16),
            V((128, 1536), BF16),
            V((2, 48, 768), BF16),
            V((2, 48, 768), BF16),
            V((8, 3072), F32),
            V((4, 1, 3072), F32),
            V((3, 4, 1, 3072), F32),
            pltpu.SemaphoreType.DMA((N_SEM,)),
            pltpu.SemaphoreType.DMA((N_SEM,)),
            pltpu.SemaphoreType.DMA((10,)),
            pltpu.SemaphoreType.DMA((4,)),
        ],
        compiler_params=pltpu.CompilerParams(
            collective_id=0, has_side_effects=True, vmem_limit_bytes=62 * 1024 * 1024
        ),
    )(
        inputs,
        norm_gain.reshape(1, 3072),
        w_qkv.reshape(4, 48, 2304),
        w_out,
        own_ids.reshape(1, 256),
        cotangent,
    )
    branch, gin, gain, gqkv, gout = pl.pallas_call(
        copy_out,
        out_shape=tuple(jax.ShapeDtypeStruct(o.shape, o.dtype) for o in outs),
        in_specs=[hbm] * 5,
        out_specs=(hbm,) * 5,
        scratch_shapes=[V(o.shape, o.dtype) for o in outs] + [pltpu.SemaphoreType.DMA((2, 5))],
    )(*outs)
    return (
        branch, gin, gain.reshape(3072),
        gqkv.reshape(192, 2304), gout,
    )


def solution(mesh):
    placed = (
        P(("depth", "col"), "row"),
        P("row"),
        P(("row", "depth"), "col"),
        P(("col", "depth"), "row"),
        P("depth", "row"),
        P(("depth", "col"), "row"),
    )
    return jax.shard_map(
        shards,
        mesh=mesh,
        in_specs=placed,
        out_specs=(
            P(("depth", "col"), "row"),
            P(("depth", "col"), "row"),
            P("row"),
            P(("row", "depth"), "col"),
            P(("col", "depth"), "row"),
        ),
        check_vma=False,
    )
```
